128 devices in a mesh: frames: 16 (over y, z_hi, core), mp: 8 (over z_lo, x).
Axes of the slice: x: 4, y: 4, z: 4 (z_hi: 2, z_lo: 2; z = z_hi * 2 + z_lo), core: 2. Of those that a mesh axis runs over, the one named last changes fastest.
Arguments:
- teacher_states: bfloat16 [65536, 1024], P('frames', 'mp'), may hold values from -6 to 6
- teacher_pred: bfloat16 [16384, 1024], P(('frames', 'mp')), may hold values from -6 to 6
- teacher_out: bfloat16 [1024, 1024], replicated, may hold values from -0.9 to 0.9
- student_states: bfloat16 [65536, 512], P(('frames', 'mp')), may hold values from -6 to 6
- embed_last: bfloat16 [1024, 512], replicated, may hold values from -4.1875 to 4.1875
- embed_second: bfloat16 [1024, 512], replicated, may hold values from -4.1875 to 4.1875
- student_out: bfloat16 [512, 1024], replicated, may hold values from -1.26 to 1.26
- labels: int32 [16384], P(('frames', 'mp')), may hold values from 1 to 1023
- label_utt: int32 [16384], P(('frames', 'mp')), may hold values from 0 to 340, never falling along the last dimension, each value on 1 to 96 neighbouring positions
- band_start: int32 [2048], P(('frames', 'mp')), may hold values from 0 to 124, as said below
- block_list: int32 [128, 16], P(('frames', 'mp')), may hold values from 0 to 2047, as said below
Outputs:
- divergence: float32 [2048, 4, 32], P(('frames', 'mp'))
The draws below stay inside these ranges and needn't reach their ends.
Inputs may be any that keep to these rules, and one draw needn't show every extreme that they name: `band_start`: within a device the starts do not fall from block to block. `block_list`: every block is listed exactly once; an owner lists only blocks of devices with its own mp index; at most 2 blocks of one device are listed by one owner, and some owner lists 2 from one device.
All inputs are finite; a program needn't handle non-finite values.
Results may differ from the reference program's by a relative error of at most 0.0045.
Values may be sent and summed in bfloat16 or wider, within the bound.
No kernel may reach another device: no remote copies, remote signals or barrier semaphores. Data moves between devices by JAX's collectives and lax.ppermute only.
A program may use at most 128 MiB of HBM per device.

```python
import math
import jax
import jax.numpy as jnp
import numpy as np
from jax import lax

V = 1024
JT = 1024
JS = 512
S = 4
BLK = 32
NB_DEV = 16
LAB_DEV = 128
NBLK = 2048
NF = 65536
NLAB = 16384
N_FRAMES = 16
N_MP = 8
DEVICES = 128


def drawn_states(key, rows, width):
    key_base = jax.random.fold_in(key, 0)
    values = jnp.clip(jax.random.normal(key_base, (rows, width)), -6.0, 6.0)
    return values.astype(jnp.bfloat16)


def drawn_weight(key, width, scale):
    key_base = jax.random.fold_in(key, 0)
    values = jnp.clip(jax.random.normal(key_base, (width, V)) * scale, -6.0 * scale, 6.0 * scale)
    return values.astype(jnp.bfloat16)


def draw_teacher_states(key, part):
    key = jax.random.fold_in(key, 1)
    return drawn_states(key, NF, JT)


def draw_teacher_out(key, part):
    key = jax.random.fold_in(key, 2)
    return drawn_weight(key, JT, 0.15)


def draw_student_states(key, part):
    key = jax.random.fold_in(key, 3)
    return drawn_states(key, NF, JS)


def draw_student_out(key, part):
    key = jax.random.fold_in(key, 4)
    return drawn_weight(key, JS, 0.21)


def draw_band_start(key, part):
    key = jax.random.fold_in(key, 5)
    highest = LAB_DEV - S
    values = jax.random.randint(key, (DEVICES, NB_DEV), 0, highest + 1)
    values = jnp.sort(values, axis=1)
    values = values.at[0, 0].set(0)
    values = values.at[0, NB_DEV - 1].set(highest)
    return values.reshape(NBLK).astype(jnp.int32)


def draw_block_list(key, part):
    key = jax.random.fold_in(key, 7)
    key_perm, key_shift, key_order = jax.random.split(key, 3)
    frame_perms = jax.vmap(lambda sub_key: jax.random.permutation(sub_key, N_FRAMES))(jax.random.split(key_perm, N_MP))
    spare_shifts = jnp.concatenate([jnp.arange(1, N_FRAMES), jnp.arange(1, N_FRAMES)]).astype(jnp.int32)
    spare_shifts = jax.random.permutation(key_shift, spare_shifts)
    shifts = jnp.concatenate([jnp.zeros((2,), jnp.int32), spare_shifts[:NB_DEV - 2]])
    owner_frame = jnp.arange(N_FRAMES, dtype=jnp.int32)
    source_frame = frame_perms[:, (owner_frame[:, None] + shifts[None, :]) % N_FRAMES]
    source_dev = source_frame * N_MP + jnp.arange(N_MP, dtype=jnp.int32)[:, None, None]
    block_ids = source_dev * NB_DEV + jnp.arange(NB_DEV, dtype=jnp.int32)[None, None, :]
    block_ids = jnp.transpose(block_ids, (1, 0, 2)).reshape(N_FRAMES * N_MP, NB_DEV)
    block_ids = jax.random.permutation(key_order, block_ids, axis=1, independent=True)
    return block_ids.astype(jnp.int32)


def place_ends(drawn, key, smallest, top_value):
    longest = drawn.shape.index(max(drawn.shape))
    spots = []
    for shift in (0, 1):
        where = [jax.random.randint(jax.random.fold_in(key, axis), (), 0, length) for axis, length in enumerate(drawn.shape)]
        where[longest] = (where[longest] + shift) % drawn.shape[longest]
        spots.append(tuple(where))
    return drawn.at[spots[0]].set(smallest).at[spots[1]].set(top_value)


def level_of(key, shape, shards, least, high):
    factor_of = 1.0
    for axis_at, blocks in shards:
        draws = jax.random.uniform(jax.random.fold_in(jax.random.fold_in(key, 6), axis_at), (blocks,), jnp.float32, least / len(shards), high / len(shards))
        factor_of = factor_of * jnp.repeat(jnp.exp(draws), shape[axis_at] // blocks).reshape((-1,) + (1,) * (len(shape) - 1 - axis_at))
    return factor_of


def profile(amount, total, reach, slope):
    loads = [(1 << 20) // math.isqrt(grade ** slope) + 1 for grade in range(2, amount + 1)]
    surplus, holding = total - reach - (amount - 1), [1] * (amount - 1)
    while surplus > 0:
        free = [i for i in range(amount - 1) if holding[i] < reach]
        pool, remaining = sum([loads[i] for i in free]), surplus
        for i in free:
            more = min(reach - holding[i], max(1, remaining * loads[i] // pool), surplus)
            holding[i] = holding[i] + more
            surplus = surplus - more
    return np.array([reach] + holding)


def uneven_parts(rng, amount, total, bound, slope):
    if amount == 2:
        one = jax.random.randint(rng, (), max(1, total - bound), min(bound, total - 1) + 1)
        return jnp.stack([one, total - one])
    lengths = jnp.asarray(profile(amount, total, bound, slope), jnp.int32)
    twos = (amount - 1) // 2
    giver, sink = lengths[1:1 + 2 * twos:2], lengths[2:2 + 2 * twos:2]
    margin = jnp.minimum(giver - 1, bound - sink)
    passed = jax.random.randint(jax.random.fold_in(rng, 1), (twos,), 0, 1 << 20) % (margin + 1)
    lengths = lengths.at[1:1 + 2 * twos:2].set(giver - passed).at[2:2 + 2 * twos:2].set(sink + passed)
    return lengths[jax.random.permutation(jax.random.fold_in(rng, 2), amount)]


def noise(key, extent, deviation, limit, cuts=(), kind=jnp.bfloat16):
    loudness = level_of(key, extent, cuts, -0.22, 0.18) if cuts else 1.0
    values = jax.random.normal(key, extent, jnp.float32) * deviation * loudness
    return jnp.minimum(jnp.maximum(values, -limit), limit).astype(kind)


def setup_inputs(seed: int = 0) -> dict:
    splits = jax.random.split(jax.random.key(seed), 12)
    teacher_states = draw_teacher_states(jax.random.fold_in(splits[11], 71), 0)
    teacher_pred = noise(splits[1], (NLAB, JT), 1.0, 6.0, ((0, 128),))
    teacher_out = draw_teacher_out(jax.random.fold_in(splits[11], 71), 0)
    student_states = draw_student_states(jax.random.fold_in(splits[11], 71), 0)
    embed_last = noise(splits[4], (V, JS), 0.7, 4.1875)
    embed_second = noise(splits[5], (V, JS), 0.7, 4.1875)
    student_out = draw_student_out(jax.random.fold_in(splits[11], 71), 0)
    labels = place_ends(jax.random.randint(splits[7], (NLAB,), 1, V), jax.random.fold_in(splits[7], 1), 1, V - 1).astype(jnp.int32)
    label_utt = jnp.searchsorted(jnp.cumsum(uneven_parts(splits[8], NLAB // 48, NLAB, 96, 1)), jnp.arange(NLAB), side="right").astype(jnp.int32)
    band_start = draw_band_start(jax.random.fold_in(splits[11], 71), 0)
    block_list = draw_block_list(jax.random.fold_in(splits[11], 71), 0)
    return dict(teacher_states=teacher_states, teacher_pred=teacher_pred, teacher_out=teacher_out, student_states=student_states, embed_last=embed_last, embed_second=embed_second, student_out=student_out, labels=labels, label_utt=label_utt, band_start=band_start, block_list=block_list)


def log_probs(logits):
    largest = jnp.max(logits, axis=-1, keepdims=True)
    shifted = logits - largest
    return shifted - jnp.log(jnp.sum(jnp.exp(shifted), axis=-1, keepdims=True))


def band_log_probs(states, band_pred, weight):
    joint_act = jnp.tanh(states[:, None, :, :].astype(jnp.float32) + band_pred[:, :, None, :].astype(jnp.float32)).astype(jnp.bfloat16)
    logits = jnp.dot(joint_act.reshape(-1, joint_act.shape[-1]), weight, preferred_element_type=jnp.float32)
    return log_probs(logits).reshape(joint_act.shape[0], joint_act.shape[1], joint_act.shape[2], weight.shape[1])


def kl_terms(teacher_logp, student_logp):
    teacher_f32 = teacher_logp.astype(jnp.float32)
    return jnp.sum(jnp.exp(teacher_f32) * (teacher_f32 - student_logp), axis=-1)


def reference(teacher_states, teacher_pred, teacher_out, student_states, embed_last, embed_second, student_out, labels, label_utt, band_start, block_list):
    zero_pad = jnp.zeros((2,), jnp.int32)
    no_utt = jnp.full((2,), -1, jnp.int32)
    padded_labels = jnp.concatenate([zero_pad, labels])
    padded_utts = jnp.concatenate([no_utt, label_utt])
    label_count = labels.shape[0]
    last_ctx = jnp.where(padded_utts[1:label_count + 1] == label_utt, padded_labels[1:label_count + 1], 0).astype(jnp.int32)
    second_ctx = jnp.where(padded_utts[:label_count] == label_utt, padded_labels[:label_count], 0).astype(jnp.int32)
    student_pred = (embed_last[last_ctx].astype(jnp.float32) + embed_second[second_ctx].astype(jnp.float32)).astype(jnp.bfloat16)
    frame_steps = jnp.arange(BLK, dtype=jnp.int32)
    band_steps = jnp.arange(S, dtype=jnp.int32)
    owner_student = student_states.reshape(DEVICES, NB_DEV, BLK, JS)

    def per_owner(items):
        my_list, my_student = items
        my_list = my_list.astype(jnp.int32)
        source_dev = my_list // NB_DEV
        frame_rows = (my_list[:, None] * BLK + frame_steps[None, :]).astype(jnp.int32)
        band_rows = (source_dev[:, None] * LAB_DEV + band_start[my_list][:, None] + band_steps[None, :]).astype(jnp.int32)
        teacher_logp = band_log_probs(teacher_states[frame_rows], teacher_pred[band_rows], teacher_out).astype(jnp.bfloat16)
        student_logp = band_log_probs(my_student, student_pred[band_rows], student_out)
        return kl_terms(teacher_logp, student_logp)

    divergence_all = lax.map(per_owner, (block_list, owner_student))
    return divergence_all.reshape(NBLK, S, BLK)
```

```python
import jax
import jax.numpy as jnp
from jax import lax
from jax.experimental import pallas as pl
from jax.experimental.pallas import tpu as pltpu
from jax.sharding import PartitionSpec as P

S = 4
CAP = 2
LANES = 128
TAG_ROWS = 16
GROUP = 4
BF16 = jnp.bfloat16
F32 = jnp.float32


def shifted_2(block, axis, distance):
    devices = range(lax.axis_size(axis))
    route = [(i - distance, i) for i in devices if i - distance in devices]
    return lax.ppermute(block, axis, route)


def by_lanes(pred):
    return pred.astype(F32).reshape(pred.shape[0], -1, LANES)


def vmem():
    return pl.BlockSpec(memory_space=pltpu.VMEM)


def smem():
    return pl.BlockSpec(memory_space=pltpu.SMEM)


def pack(block_list, student_states, frame_peers, blocks_per_peer):
    count = block_list.shape[1]
    rows, width = student_states.shape
    block_rows = rows // count
    pieces = width // LANES
    slot_rows = block_rows * pieces
    message = CAP * slot_rows + TAG_ROWS

    def body(list_ref, states_ref, out_ref, used):
        lane = lax.broadcasted_iota(jnp.int32, (TAG_ROWS, LANES), 1)
        for peer in range(frame_peers):
            used[peer] = 0
            out_ref[peer, CAP * slot_rows :, :] = jnp.full((TAG_ROWS, LANES), -1.0, BF16)
        for j in range(count):
            block = list_ref[0, j]
            peer = block // blocks_per_peer
            slot = used[peer]
            used[peer] = slot + 1
            local = block % count
            for piece in range(pieces):
                at = pl.multiple_of(slot * slot_rows + piece * block_rows, TAG_ROWS)
                out_ref[peer, pl.ds(at, block_rows), :] = states_ref[
                    j * block_rows : (j + 1) * block_rows, piece * LANES : (piece + 1) * LANES
                ]
            tags = out_ref[peer, CAP * slot_rows :, :].astype(F32)
            tags = jnp.where(lane == slot, local.astype(F32), tags)
            out_ref[peer, CAP * slot_rows :, :] = tags.astype(BF16)

    return pl.pallas_call(
        body,
        out_shape=jax.ShapeDtypeStruct((frame_peers, message, LANES), BF16),
        in_specs=[smem(), vmem()],
        out_specs=vmem(),
        scratch_shapes=[pltpu.SMEM((frame_peers,), jnp.int32)],
        compiler_params=pltpu.CompilerParams(vmem_limit_bytes=60 << 20),
        cost_estimate=pl.CostEstimate(flops=0, bytes_accessed=3 << 20, transcendentals=0),
        name="pack",
    )(block_list, student_states)


def teacher(relaid, teacher_pred, teacher_out, band_start):
    pieces, rows, _ = relaid.shape
    count = band_start.shape[0]
    width, vocab = teacher_out.shape
    block_rows = rows // count
    out_block = S * block_rows
    step_rows = GROUP * out_block

    def body(start_ref, states_ref, pred_ref, weight_ref, e_ref, stat_ref, act):
        step = pl.program_id(0)
        for local in range(GROUP):
            first = start_ref[step * GROUP + local]
            for piece in range(pieces):
                cols = slice(piece * LANES, (piece + 1) * LANES)
                states = states_ref[piece, local * block_rows : (local + 1) * block_rows, :].astype(F32)
                for k in range(S):
                    at = local * out_block + k * block_rows
                    band = pred_ref[first + k, piece : piece + 1, :]
                    act[at : at + block_rows, cols] = jnp.tanh(states + band).astype(BF16)
        logits = jnp.dot(act[...], weight_ref[...], preferred_element_type=F32)
        shifted = logits - jnp.max(logits, axis=-1, keepdims=True)
        e = jnp.exp(shifted)
        e_ref[...] = e
        total = jnp.sum(e, axis=-1, keepdims=True)
        weighted = jnp.sum(e * shifted, axis=-1, keepdims=True)
        lane = lax.broadcasted_iota(jnp.int32, (step_rows, LANES), 1)
        inverse = 1.0 / total
        stat_ref[...] = jnp.where(lane == 0, inverse, weighted * inverse - jnp.log(total))

    return pl.pallas_call(
        body,
        grid=(count // GROUP,),
        out_shape=(
            jax.ShapeDtypeStruct((count * out_block, vocab), F32),
            jax.ShapeDtypeStruct((count * out_block, LANES), F32),
        ),
        in_specs=[
            smem(),
            pl.BlockSpec((pieces, GROUP * block_rows, LANES), lambda i: (0, i, 0)),
            pl.BlockSpec(teacher_pred.shape, lambda i: (0, 0, 0)),
            pl.BlockSpec((width, vocab), lambda i: (0, 0)),
        ],
        out_specs=(
            pl.BlockSpec((step_rows, vocab), lambda i: (i, 0)),
            pl.BlockSpec((step_rows, LANES), lambda i: (i, 0)),
        ),
        scratch_shapes=[pltpu.VMEM((step_rows, width), BF16)],
        compiler_params=pltpu.CompilerParams(vmem_limit_bytes=60 << 20),
        cost_estimate=pl.CostEstimate(
            flops=2 * count * out_block * width * vocab,
            bytes_accessed=14 << 20,
            transcendentals=count * out_block * (width + vocab),
        ),
        name="teacher",
    )(band_start, relaid, teacher_pred, teacher_out)


def student(arrived, student_pred, student_out, band_start, e, stats):
    peers, message, _ = arrived.shape
    count = band_start.shape[0]
    width, vocab = student_out.shape
    pieces = width // LANES
    slot_rows = (message - TAG_ROWS) // CAP
    block_rows = slot_rows // pieces
    out_block = S * block_rows
    step_rows = GROUP * out_block
    assert out_block == LANES

    def body(
        start_ref, arrived_ref, pred_ref, weight_ref, e_ref, stat_ref, out_ref,
        act, tags, tag_smem, where, answers, sem,
    ):
        step = pl.program_id(0)

        @pl.when(step == 0)
        def _():
            for peer in range(peers):
                tile = arrived_ref[peer, CAP * slot_rows :, :].astype(F32)
                tags[peer : peer + 1, :] = tile[:1, :].astype(jnp.int32)
            copy = pltpu.make_async_copy(tags, tag_smem, sem)
            copy.start()
            copy.wait()
            for peer in range(peers):
                for slot in range(CAP):
                    block = tag_smem[peer, slot]
                    where[jnp.where(block < 0, count, block)] = peer * CAP + slot

        for local in range(GROUP):
            block = step * GROUP + local
            first = start_ref[block]
            place = where[block]
            peer = place // CAP
            slot = place % CAP
            for piece in range(pieces):
                cols = slice(piece * LANES, (piece + 1) * LANES)
                at = pl.multiple_of(slot * slot_rows + piece * block_rows, TAG_ROWS)
                states = arrived_ref[peer, pl.ds(at, block_rows), :].astype(F32)
                for k in range(S):
                    at = local * out_block + k * block_rows
                    band = pred_ref[first + k, piece : piece + 1, :]
                    act[at : at + block_rows, cols] = jnp.tanh(states + band).astype(BF16)
        logits = jnp.dot(act[...], weight_ref[...], preferred_element_type=F32)
        shifted = logits - jnp.max(logits, axis=-1, keepdims=True)
        total = jnp.sum(jnp.exp(shifted), axis=-1, keepdims=True)
        cross = jnp.sum(e_ref[...] * shifted, axis=-1, keepdims=True)
        answer = stat_ref[:, 1:2] - cross * stat_ref[:, 0:1] + jnp.log(total)
        lane = lax.broadcasted_iota(jnp.int32, (LANES, LANES), 1)
        for local in range(GROUP):
            column = answer[local * out_block : (local + 1) * out_block, :]
            answers[...] = jnp.where(lane == step * GROUP + local, column, answers[...])

        @pl.when(step == count // GROUP - 1)
        def _():
            answers[...] = answers[...].T
            for block in range(count):
                place = where[block]
                out_ref[place // CAP, place % CAP] = jnp.broadcast_to(answers[block : block + 1, :], (8, LANES))

    return pl.pallas_call(
        body,
        grid=(count // GROUP,),
        out_shape=jax.ShapeDtypeStruct((peers, CAP, 8, LANES), F32),
        in_specs=[
            smem(),
            pl.BlockSpec((peers, message, LANES), lambda i: (0, 0, 0)),
            pl.BlockSpec(student_pred.shape, lambda i: (0, 0, 0)),
            pl.BlockSpec((width, vocab), lambda i: (0, 0)),
            pl.BlockSpec((step_rows, vocab), lambda i: (i, 0)),
            pl.BlockSpec((step_rows, LANES), lambda i: (i, 0)),
        ],
        out_specs=pl.BlockSpec((peers, CAP, 8, LANES), lambda i: (0, 0, 0, 0)),
        scratch_shapes=[
            pltpu.VMEM((step_rows, width), BF16),
            pltpu.VMEM((peers, LANES), jnp.int32),
            pltpu.SMEM((peers, LANES), jnp.int32),
            pltpu.SMEM((count + 1,), jnp.int32),
            pltpu.VMEM((LANES, LANES), F32),
            pltpu.SemaphoreType.DMA,
        ],
        compiler_params=pltpu.CompilerParams(vmem_limit_bytes=60 << 20),
        cost_estimate=pl.CostEstimate(
            flops=2 * count * out_block * width * vocab,
            bytes_accessed=12 << 20,
            transcendentals=count * out_block * (width + vocab),
        ),
        name="student",
    )(band_start, arrived, student_pred, student_out, e, stats)


def pick(block_list, answers, blocks_per_peer, block_rows):
    count = block_list.shape[1]
    peers = answers.shape[0]

    def body(list_ref, answers_ref, out_ref, used, rows):
        for peer in range(peers):
            used[peer] = 0
        for j in range(count):
            peer = list_ref[0, j] // blocks_per_peer
            slot = used[peer]
            used[peer] = slot + 1
            rows[j : j + 1, :] = answers_ref[peer, slot, :1, :]
        for k in range(S):
            out_ref[:, k, :] = rows[:, k * block_rows : (k + 1) * block_rows]

    return pl.pallas_call(
        body,
        out_shape=jax.ShapeDtypeStruct((count, S, block_rows), F32),
        in_specs=[smem(), vmem()],
        out_specs=vmem(),
        scratch_shapes=[pltpu.SMEM((peers,), jnp.int32), pltpu.VMEM((count, LANES), F32)],
        compiler_params=pltpu.CompilerParams(vmem_limit_bytes=60 << 20),
        name="pick",
    )(block_list, answers)


def shards(
    teacher_states,
    teacher_pred,
    teacher_out,
    student_states,
    embed_last,
    embed_second,
    student_out,
    labels,
    label_utt,
    band_start,
    block_list,
):
    block_count = band_start.shape[0]
    block_rows = student_states.shape[0] // block_count
    frame_peers = lax.axis_size("frames")
    mp_peers = lax.axis_size("mp")
    blocks_per_peer = block_count * mp_peers

    relaid = lax.all_to_all(
        teacher_states.reshape(mp_peers, -1, teacher_states.shape[1]), "mp", split_axis=0, concat_axis=0
    )
    outgoing = pack(block_list, student_states, frame_peers, blocks_per_peer)
    arrived = lax.all_to_all(outgoing, "frames", split_axis=0, concat_axis=0)

    neighbour = shifted_2(jnp.stack([labels[-2:], label_utt[-2:]]), ("frames", "mp"), 1)
    padded_labels = jnp.concatenate([neighbour[0], labels])
    padded_utts = jnp.concatenate([neighbour[1], label_utt])
    label_count = labels.shape[0]
    last_ctx = jnp.where(
        padded_utts[1 : label_count + 1] == label_utt, padded_labels[1 : label_count + 1], 0
    )
    second_ctx = jnp.where(padded_utts[:label_count] == label_utt, padded_labels[:label_count], 0)
    vocab_ids = jnp.arange(embed_last.shape[0], dtype=jnp.int32)
    last_hot = (last_ctx[:, None] == vocab_ids[None, :]).astype(BF16)
    second_hot = (second_ctx[:, None] == vocab_ids[None, :]).astype(BF16)
    student_pred = (
        jnp.dot(last_hot, embed_last, preferred_element_type=F32)
        + jnp.dot(second_hot, embed_second, preferred_element_type=F32)
    ).astype(BF16)

    e, stats = teacher(relaid, by_lanes(teacher_pred), teacher_out, band_start)
    answers = student(arrived, by_lanes(student_pred), student_out, band_start, e, stats)
    returned = lax.all_to_all(answers, "frames", split_axis=0, concat_axis=0)
    return pick(block_list, returned, blocks_per_peer, block_rows)


def solution(mesh):
    placed = (
        P("frames", "mp"),
        P(("frames", "mp"), None),
        P(),
        P(("frames", "mp"), None),
        P(),
        P(),
        P(),
        P(("frames", "mp")),
        P(("frames", "mp")),
        P(("frames", "mp")),
        P(("frames", "mp"), None),
    )
    return jax.shard_map(
        shards,
        mesh=mesh,
        in_specs=placed,
        out_specs=P(("frames", "mp"), None, None),
        check_vma=False,
    )
```

```python
import jax
import jax.numpy as jnp
from jax import lax
from jax.experimental import pallas as pl
from jax.experimental.pallas import tpu as pltpu
from jax.sharding import PartitionSpec as P

S = 4
CAP = 2
LANES = 128
TAG_ROWS = 16
GROUP = 2
BF16 = jnp.bfloat16
F32 = jnp.float32


def shifted_2(block, axis, distance):
    devices = range(lax.axis_size(axis))
    route = [(i - distance, i) for i in devices if i - distance in devices]
    return lax.ppermute(block, axis, route)


def by_lanes(pred):
    return pred.astype(F32).reshape(pred.shape[0], -1, LANES)


def vmem():
    return pl.BlockSpec(memory_space=pltpu.VMEM)


def hbm():
    return pl.BlockSpec(memory_space=pltpu.HBM)


def anywhere():
    return pl.BlockSpec(memory_space=pl.ANY)


def smem():
    return pl.BlockSpec(memory_space=pltpu.SMEM)


def pack(block_list, student_states, frame_peers, blocks_per_peer):
    count = block_list.shape[1]
    rows, width = student_states.shape
    block_rows = rows // count
    pieces = width // LANES
    slot_rows = block_rows * pieces
    message = CAP * slot_rows + TAG_ROWS

    def body(list_ref, states_ref, out_ref, used):
        lane = lax.broadcasted_iota(jnp.int32, (TAG_ROWS, LANES), 1)
        for peer in range(frame_peers):
            used[peer] = 0
            out_ref[peer, CAP * slot_rows :, :] = jnp.full((TAG_ROWS, LANES), -1.0, BF16)
        for j in range(count):
            block = list_ref[0, j]
            peer = block // blocks_per_peer
            slot = used[peer]
            used[peer] = slot + 1
            local = block % count
            for piece in range(pieces):
                at = pl.multiple_of(slot * slot_rows + piece * block_rows, TAG_ROWS)
                out_ref[peer, pl.ds(at, block_rows), :] = states_ref[
                    j * block_rows : (j + 1) * block_rows, piece * LANES : (piece + 1) * LANES
                ]
            tags = out_ref[peer, CAP * slot_rows :, :].astype(F32)
            tags = jnp.where(lane == slot, local.astype(F32), tags)
            out_ref[peer, CAP * slot_rows :, :] = tags.astype(BF16)

    return pl.pallas_call(
        body,
        out_shape=jax.ShapeDtypeStruct((frame_peers, message, LANES), BF16),
        in_specs=[smem(), vmem()],
        out_specs=vmem(),
        scratch_shapes=[pltpu.SMEM((frame_peers,), jnp.int32)],
        compiler_params=pltpu.CompilerParams(vmem_limit_bytes=4 << 20),
        cost_estimate=pl.CostEstimate(flops=0, bytes_accessed=3 << 20, transcendentals=0),
        name="pack",
    )(block_list, student_states)


def teacher(relaid, teacher_pred, teacher_out, student_out_t, band_start):
    pieces, rows, _ = relaid.shape
    count = band_start.shape[0]
    width, vocab = teacher_out.shape
    student_width = student_out_t.shape[1]
    block_rows = rows // count
    out_block = S * block_rows
    step_rows = GROUP * out_block
    steps = count // GROUP
    total_rows = count * out_block

    def body(start_ref, states_ref, pred_ref, weight_ref, student_ref, q_ref, stat_ref, act, logits, e, inverse, sums, cross):
        lane = lax.broadcasted_iota(jnp.int32, (out_block, LANES), 1)

        def activate(step):
            for block in range(step * GROUP, (step + 1) * GROUP):
                first = start_ref[block]
                for piece in range(pieces):
                    cols = slice(piece * LANES, (piece + 1) * LANES)
                    states = states_ref[piece, block * block_rows : (block + 1) * block_rows, :].astype(F32)
                    for k in range(S):
                        at = block * out_block + k * block_rows
                        band = pred_ref[first + k, piece : piece + 1, :]
                        act[at : at + block_rows, cols] = jnp.tanh(states + band).astype(BF16)

        def multiply(step):
            at = slice(step * step_rows, (step + 1) * step_rows)
            logits[at, :] = jnp.dot(act[at, :], weight_ref[...], preferred_element_type=F32)

        def normalise(step):
            for block in range(step * GROUP, (step + 1) * GROUP):
                at = slice(block * out_block, (block + 1) * out_block)
                values = logits[at, :]
                shifted = values - jnp.max(values, axis=-1, keepdims=True)
                exps = jnp.exp(shifted)
                e[at, :] = exps.astype(BF16)
                total = jnp.sum(exps, axis=-1, keepdims=True)
                weighted = jnp.sum(exps * shifted, axis=-1, keepdims=True)
                inverse[at, :] = jnp.broadcast_to(1.0 / total, (out_block, LANES))
                sums[...] = jnp.where(lane == block, total, sums[...])
                cross[...] = jnp.where(lane == block, weighted, cross[...])

        def project(step):
            at = slice(step * step_rows, (step + 1) * step_rows)
            product = jnp.dot(e[at, :], student_ref[...], preferred_element_type=F32)
            scale = inverse[at, :]
            for piece in range(student_width // LANES):
                cols = slice(piece * LANES, (piece + 1) * LANES)
                q_ref[at, cols] = (product[:, cols] * scale).astype(BF16)

        for step in range(steps + 3):
            for delay, part in enumerate((activate, multiply, normalise, project)):
                if 0 <= step - delay < steps:
                    part(step - delay)
        total = sums[...].T[:count]
        stat_ref[...] = cross[...].T[:count] / total - jnp.log(total)

    return pl.pallas_call(
        body,
        out_shape=(
            jax.ShapeDtypeStruct((total_rows, student_width), BF16),
            jax.ShapeDtypeStruct((count, out_block), F32),
        ),
        in_specs=[smem(), vmem(), vmem(), vmem(), vmem()],
        out_specs=(vmem(), vmem()),
        scratch_shapes=[
            pltpu.VMEM((total_rows, width), BF16),
            pltpu.VMEM((total_rows, vocab), F32),
            pltpu.VMEM((total_rows, vocab), BF16),
            pltpu.VMEM((total_rows, LANES), F32),
            pltpu.VMEM((out_block, LANES), F32),
            pltpu.VMEM((out_block, LANES), F32),
        ],
        compiler_params=pltpu.CompilerParams(vmem_limit_bytes=56 << 20),
        cost_estimate=pl.CostEstimate(
            flops=2 * total_rows * (width + student_width) * vocab,
            bytes_accessed=8 << 20,
            transcendentals=total_rows * (width + vocab),
        ),
        name="teacher",
    )(band_start, relaid, teacher_pred, teacher_out, student_out_t)


def student(arrived, student_pred, student_out, band_start, q, stats):
    peers, message, _ = arrived.shape
    count = band_start.shape[0]
    width, vocab = student_out.shape
    pieces = width // LANES
    slot_rows = (message - TAG_ROWS) // CAP
    block_rows = slot_rows // pieces
    out_block = S * block_rows
    step_rows = GROUP * out_block
    steps = count // GROUP
    total_rows = count * out_block
    assert out_block == LANES

    def body(
        start_ref, arrived_ref, pred_hbm, weight_hbm, q_hbm, stat_ref, out_ref,
        act, logits, products, pred_ref, weight_ref, q_ref, tags, tag_smem, where, sums, cross, sems,
    ):
        lane = lax.broadcasted_iota(jnp.int32, (out_block, LANES), 1)
        copies = [
            pltpu.make_async_copy(pred_hbm, pred_ref, sems.at[1]),
            pltpu.make_async_copy(weight_hbm, weight_ref, sems.at[2]),
            pltpu.make_async_copy(q_hbm, q_ref, sems.at[3]),
        ]
        for each in copies:
            each.start()
        for peer in range(peers):
            tile = arrived_ref[peer, CAP * slot_rows :, :].astype(F32)
            tags[peer : peer + 1, :] = tile[:1, :].astype(jnp.int32)
        copy = pltpu.make_async_copy(tags, tag_smem, sems.at[0])
        copy.start()
        copy.wait()
        for peer in range(peers):
            for slot in range(CAP):
                block = tag_smem[peer, slot]
                where[jnp.where(block < 0, count, block)] = peer * CAP + slot

        for each in copies:
            each.wait()

        def activate(step):
            for block in range(step * GROUP, (step + 1) * GROUP):
                first = start_ref[block]
                place = where[block]
                peer = place // CAP
                slot = place % CAP
                terms = [None] * S
                for piece in range(pieces):
                    cols = slice(piece * LANES, (piece + 1) * LANES)
                    at = pl.multiple_of(slot * slot_rows + piece * block_rows, TAG_ROWS)
                    states = arrived_ref[peer, pl.ds(at, block_rows), :].astype(F32)
                    for k in range(S):
                        at = block * out_block + k * block_rows
                        band = pred_ref[first + k, piece : piece + 1, :]
                        values = jnp.tanh(states + band).astype(BF16)
                        act[at : at + block_rows, cols] = values
                        term = values.astype(F32) * q_ref[at : at + block_rows, cols].astype(F32)
                        terms[k] = term if terms[k] is None else terms[k] + term
                for k in range(S):
                    at = block * out_block + k * block_rows
                    products[at : at + block_rows, :] = terms[k]

        def multiply(step):
            at = slice(step * step_rows, (step + 1) * step_rows)
            logits[at, :] = jnp.dot(act[at, :], weight_ref[...], preferred_element_type=F32)

        def normalise(step):
            for block in range(step * GROUP, (step + 1) * GROUP):
                at = slice(block * out_block, (block + 1) * out_block)
                values = logits[at, :]
                largest = jnp.max(values, axis=-1, keepdims=True)
                total = jnp.sum(jnp.exp(values - largest), axis=-1, keepdims=True)
                mixed = jnp.sum(products[at, :], axis=-1, keepdims=True)
                sums[...] = jnp.where(lane == block, total, sums[...])
                cross[...] = jnp.where(lane == block, largest - mixed, cross[...])

        for step in range(steps + 2):
            for delay, part in enumerate((activate, multiply, normalise)):
                if 0 <= step - delay < steps:
                    part(step - delay)
        answers = stat_ref[...] + cross[...].T[:count] + jnp.log(sums[...].T[:count])
        for block in range(count):
            place = where[block]
            out_ref[place // CAP, place % CAP] = jnp.broadcast_to(answers[block : block + 1, :], (8, LANES))

    return pl.pallas_call(
        body,
        out_shape=jax.ShapeDtypeStruct((peers, CAP, 8, LANES), F32),
        in_specs=[smem(), vmem(), anywhere(), anywhere(), anywhere(), vmem()],
        out_specs=vmem(),
        scratch_shapes=[
            pltpu.VMEM((total_rows, width), BF16),
            pltpu.VMEM((total_rows, vocab), F32),
            pltpu.VMEM((total_rows, LANES), F32),
            pltpu.VMEM(student_pred.shape, F32),
            pltpu.VMEM((width, vocab), BF16),
            pltpu.VMEM((total_rows, width), BF16),
            pltpu.VMEM((peers, LANES), jnp.int32),
            pltpu.SMEM((peers, LANES), jnp.int32),
            pltpu.SMEM((count + 1,), jnp.int32),
            pltpu.VMEM((out_block, LANES), F32),
            pltpu.VMEM((out_block, LANES), F32),
            pltpu.SemaphoreType.DMA((4,)),
        ],
        compiler_params=pltpu.CompilerParams(vmem_limit_bytes=50 << 20),
        cost_estimate=pl.CostEstimate(
            flops=2 * total_rows * width * vocab,
            bytes_accessed=6 << 20,
            transcendentals=total_rows * (width + vocab),
        ),
        name="student",
    )(band_start, arrived, student_pred, student_out, q, stats)


def pick(block_list, answers, blocks_per_peer, block_rows):
    count = block_list.shape[1]
    peers = answers.shape[0]

    def body(list_ref, answers_ref, out_ref, used, rows):
        for peer in range(peers):
            used[peer] = 0
        for j in range(count):
            peer = list_ref[0, j] // blocks_per_peer
            slot = used[peer]
            used[peer] = slot + 1
            rows[j : j + 1, :] = answers_ref[peer, slot, :1, :]
        for k in range(S):
            out_ref[:, k, :] = rows[:, k * block_rows : (k + 1) * block_rows]

    return pl.pallas_call(
        body,
        out_shape=jax.ShapeDtypeStruct((count, S, block_rows), F32),
        in_specs=[smem(), vmem()],
        out_specs=vmem(),
        scratch_shapes=[pltpu.SMEM((peers,), jnp.int32), pltpu.VMEM((count, LANES), F32)],
        compiler_params=pltpu.CompilerParams(vmem_limit_bytes=4 << 20),
        name="pick",
    )(block_list, answers)


def shards(
    teacher_states,
    teacher_pred,
    teacher_out,
    student_states,
    embed_last,
    embed_second,
    student_out,
    labels,
    label_utt,
    band_start,
    block_list,
):
    block_count = band_start.shape[0]
    block_rows = student_states.shape[0] // block_count
    frame_peers = lax.axis_size("frames")
    mp_peers = lax.axis_size("mp")
    blocks_per_peer = block_count * mp_peers

    relaid = lax.all_to_all(
        teacher_states.reshape(mp_peers, -1, teacher_states.shape[1]), "mp", split_axis=0, concat_axis=0
    )
    outgoing = pack(block_list, student_states, frame_peers, blocks_per_peer)
    arrived = lax.all_to_all(outgoing, "frames", split_axis=0, concat_axis=0)

    neighbour = shifted_2(jnp.stack([labels[-2:], label_utt[-2:]]), ("frames", "mp"), 1)
    padded_labels = jnp.concatenate([neighbour[0], labels])
    padded_utts = jnp.concatenate([neighbour[1], label_utt])
    label_count = labels.shape[0]
    last_ctx = jnp.where(
        padded_utts[1 : label_count + 1] == label_utt, padded_labels[1 : label_count + 1], 0
    )
    second_ctx = jnp.where(padded_utts[:label_count] == label_utt, padded_labels[:label_count], 0)
    vocab_ids = jnp.arange(embed_last.shape[0], dtype=jnp.int32)
    last_hot = (last_ctx[:, None] == vocab_ids[None, :]).astype(BF16)
    second_hot = (second_ctx[:, None] == vocab_ids[None, :]).astype(BF16)
    student_pred = (
        jnp.dot(last_hot, embed_last, preferred_element_type=F32)
        + jnp.dot(second_hot, embed_second, preferred_element_type=F32)
    ).astype(BF16)

    q, stats = teacher(relaid, by_lanes(teacher_pred), teacher_out, student_out.T, band_start)
    answers = student(arrived, by_lanes(student_pred), student_out, band_start, q, stats)
    returned = lax.all_to_all(answers, "frames", split_axis=0, concat_axis=0)
    return pick(block_list, returned, blocks_per_peer, block_rows)


def solution(mesh):
    placed = (
        P("frames", "mp"),
        P(("frames", "mp"), None),
        P(),
        P(("frames", "mp"), None),
        P(),
        P(),
        P(),
        P(("frames", "mp")),
        P(("frames", "mp")),
        P(("frames", "mp")),
        P(("frames", "mp"), None),
    )
    return jax.shard_map(
        shards,
        mesh=mesh,
        in_specs=placed,
        out_specs=P(("frames", "mp"), None, None),
        check_vma=False,
    )
```

```python
import jax
import jax.numpy as jnp
from jax import lax
from jax.experimental import pallas as pl
from jax.experimental.pallas import tpu as pltpu
from jax.sharding import PartitionSpec as P

S = 4
CAP = 2
LANES = 128
TAG_ROWS = 16
CORES = 2
PARTS = 3
GROUP = 2
BF16 = jnp.bfloat16
F32 = jnp.float32


def shifted_2(block, axis, distance):
    devices = range(lax.axis_size(axis))
    route = [(i - distance, i) for i in devices if i - distance in devices]
    return lax.ppermute(block, axis, route)


def by_tiles(rows, out_ref):
    for piece in range(rows.shape[1] // LANES):
        out_ref[:, piece, :] = rows[:, piece * LANES : (piece + 1) * LANES]


def vmem():
    return pl.BlockSpec(memory_space=pltpu.VMEM)


def hbm():
    return pl.BlockSpec(memory_space=pltpu.HBM)


def anywhere():
    return pl.BlockSpec(memory_space=pl.ANY)


def smem():
    return pl.BlockSpec(memory_space=pltpu.SMEM)


def pack(
    block_list, student_states, core, labels, label_utt, embed_last, embed_second, teacher_pred, student_out,
    frame_peers, blocks_per_peer,
):
    count = block_list.shape[1]
    rows, width = student_states.shape
    block_rows = rows // count
    pieces = width // LANES
    slot_rows = block_rows * pieces
    message = CAP * slot_rows + TAG_ROWS
    chips = frame_peers // CORES
    label_count = labels.shape[1]
    words = embed_last.shape[0]
    assert label_count == LANES

    def body(
        list_ref, core_ref, states_ref, labels_ref, utt_ref, last_ref, second_ref, teacher_pred_ref, student_ref,
        own_ref, other_ref, pred_ref, tiles_ref, turned_ref, used, hot,
    ):
        wide = lax.broadcasted_iota(jnp.int32, (LANES, LANES), 1)

        def embed(distance, ref):
            label = pltpu.roll(jnp.broadcast_to(labels_ref[...], (8, LANES)), distance, 1)
            utt = pltpu.roll(jnp.broadcast_to(utt_ref[...], (8, LANES)), distance, 1)
            label = jnp.where(utt == utt_ref[...], label, 0)
            label = jnp.broadcast_to(label[:1, :].astype(F32), (LANES, LANES)).T.astype(jnp.int32)
            for piece in range(words // LANES):
                cols = slice(piece * LANES, (piece + 1) * LANES)
                hot[:, cols] = (label == wide + piece * LANES).astype(F32).astype(BF16)
            return jnp.dot(hot[...], ref[...], preferred_element_type=F32)

        pred = (embed(1, last_ref) + embed(2, second_ref)).astype(BF16)
        by_tiles(pred.astype(F32), pred_ref)
        by_tiles(teacher_pred_ref[...].astype(F32), tiles_ref)
        turned_ref[...] = student_ref[...].astype(F32).T.astype(BF16)
        lane = lax.broadcasted_iota(jnp.int32, (TAG_ROWS, LANES), 1)
        for peer in range(frame_peers):
            used[peer] = 0
        for chip in range(chips):
            for out_ref in (own_ref, other_ref):
                out_ref[chip, CAP * slot_rows :, :] = jnp.full((TAG_ROWS, LANES), -1.0, BF16)
        for j in range(count):
            block = list_ref[0, j]
            peer = block // blocks_per_peer
            slot = used[peer]
            used[peer] = slot + 1
            local = block % count

            def put(out_ref):
                chip = peer // CORES
                for piece in range(pieces):
                    at = pl.multiple_of(slot * slot_rows + piece * block_rows, TAG_ROWS)
                    out_ref[chip, pl.ds(at, block_rows), :] = states_ref[
                        j * block_rows : (j + 1) * block_rows, piece * LANES : (piece + 1) * LANES
                    ]
                tags = out_ref[chip, CAP * slot_rows :, :].astype(F32)
                tags = jnp.where(lane == slot, local.astype(F32), tags)
                out_ref[chip, CAP * slot_rows :, :] = tags.astype(BF16)

            pl.when(peer % CORES == core_ref[0])(lambda: put(own_ref))
            pl.when(peer % CORES != core_ref[0])(lambda: put(other_ref))

    return pl.pallas_call(
        body,
        out_shape=(jax.ShapeDtypeStruct((chips, message, LANES), BF16),) * 2
        + (
            jax.ShapeDtypeStruct((label_count, pieces, LANES), F32),
            jax.ShapeDtypeStruct((label_count, teacher_pred.shape[1] // LANES, LANES), F32),
            jax.ShapeDtypeStruct(student_out.shape[::-1], BF16),
        ),
        in_specs=[smem(), smem()] + [vmem()] * 7,
        out_specs=(vmem(),) * 5,
        scratch_shapes=[pltpu.SMEM((frame_peers,), jnp.int32), pltpu.VMEM((label_count, words), BF16)],
        compiler_params=pltpu.CompilerParams(vmem_limit_bytes=16 << 20),
        cost_estimate=pl.CostEstimate(flops=0, bytes_accessed=3 << 20, transcendentals=0),
        name="pack",
    )(block_list, core, student_states, labels, label_utt, embed_last, embed_second, teacher_pred, student_out)


def teacher(relaid, teacher_pred, teacher_out, student_out_t, band_start):
    pieces, rows, _ = relaid.shape
    count = band_start.shape[0]
    width, vocab = teacher_out.shape
    student_width = student_out_t.shape[1]
    block_rows = rows // count
    out_block = S * block_rows
    step_rows = GROUP * out_block
    steps = count // GROUP
    total_rows = count * out_block

    def body(start_ref, states_ref, pred_ref, weight_ref, student_ref, q_ref, act, logits, e, inverse, sums, cross):
        lane = lax.broadcasted_iota(jnp.int32, (out_block, LANES), 1)

        def activate(step):
            for block in range(step * GROUP, (step + 1) * GROUP):
                first = start_ref[block]
                for piece in range(pieces):
                    cols = slice(piece * LANES, (piece + 1) * LANES)
                    states = states_ref[piece, block * block_rows : (block + 1) * block_rows, :].astype(F32)
                    for k in range(S):
                        at = block * out_block + k * block_rows
                        band = pred_ref[first + k, piece : piece + 1, :]
                        act[at : at + block_rows, cols] = jnp.tanh(states + band).astype(BF16)

        def multiply(step):
            at = slice(step * step_rows, (step + 1) * step_rows)
            logits[at, :] = jnp.dot(act[at, :], weight_ref[...], preferred_element_type=F32)

        def normalise(step):
            for block in range(step * GROUP, (step + 1) * GROUP):
                at = slice(block * out_block, (block + 1) * out_block)
                values = logits[at, :]
                shifted = values - jnp.max(values, axis=-1, keepdims=True)
                exps = jnp.exp(shifted)
                e[at, :] = exps.astype(BF16)
                total = jnp.sum(exps, axis=-1, keepdims=True)
                weighted = jnp.sum(exps * shifted, axis=-1, keepdims=True)
                inverse[at, :] = jnp.broadcast_to(1.0 / total, (out_block, LANES))
                sums[...] = jnp.where(lane == block, total, sums[...])
                cross[...] = jnp.where(lane == block, weighted, cross[...])

        def project(step):
            at = slice(step * step_rows, (step + 1) * step_rows)
            product = jnp.dot(e[at, :], student_ref[...], preferred_element_type=F32)
            scale = inverse[at, :]
            for piece in range(student_width // LANES):
                cols = slice(piece * LANES, (piece + 1) * LANES)
                q_ref[at, cols] = (product[:, cols] * scale).astype(BF16)

        for step in range(steps + 3):
            for delay, part in enumerate((activate, multiply, normalise, project)):
                if 0 <= step - delay < steps:
                    part(step - delay)
        total = sums[...].T[:count]
        rest = cross[...].T[:count] / total - jnp.log(total)
        for part in range(PARTS):
            rounded = rest.astype(BF16)
            q_ref[total_rows:, part * LANES : (part + 1) * LANES] = rounded
            rest = rest - rounded.astype(F32)

    return pl.pallas_call(
        body,
        out_shape=jax.ShapeDtypeStruct((total_rows + count, student_width), BF16),
        in_specs=[smem(), vmem(), vmem(), vmem(), vmem()],
        out_specs=vmem(),
        scratch_shapes=[
            pltpu.VMEM((total_rows, width), BF16),
            pltpu.VMEM((total_rows, vocab), F32),
            pltpu.VMEM((total_rows, vocab), BF16),
            pltpu.VMEM((total_rows, LANES), F32),
            pltpu.VMEM((out_block, LANES), F32),
            pltpu.VMEM((out_block, LANES), F32),
        ],
        compiler_params=pltpu.CompilerParams(vmem_limit_bytes=56 << 20),
        cost_estimate=pl.CostEstimate(flops=40 << 30, bytes_accessed=8 << 20, transcendentals=0),
        name="teacher",
    )(band_start, relaid, teacher_pred, teacher_out, student_out_t)


def student(
    core, arrived, student_pred, student_out, band_start, q, labels, label_utt, before, embed_last, embed_second
):
    chips, message, _ = arrived.shape
    message //= CORES
    peers = chips * CORES
    count = band_start.shape[0]
    width, vocab = student_out.shape
    pieces = width // LANES
    slot_rows = (message - TAG_ROWS) // CAP
    block_rows = slot_rows // pieces
    out_block = S * block_rows
    step_rows = GROUP * out_block
    steps = count // GROUP
    total_rows = count * out_block
    assert out_block == LANES

    def body(
        start_ref, core_ref, labels_ref, utt_ref, before_ref, arrived_ref, pred_hbm, weight_hbm, q_hbm, last_hbm, second_hbm,
        out_ref, entries,
        act, logits, pred_ref, weight_ref, q_ref, tags, tag_smem, where, sums, cross, sems,
    ):
        lane = lax.broadcasted_iota(jnp.int32, (out_block, LANES), 1)
        copies = [
            pltpu.make_async_copy(pred_hbm, pred_ref, sems.at[1]),
            pltpu.make_async_copy(weight_hbm, weight_ref, sems.at[2]),
            pltpu.make_async_copy(q_hbm, q_ref, sems.at[3]),
        ]
        words = []
        for at in range(2):
            for distance, table in ((1, last_hbm), (2, second_hbm)):
                i = at - distance
                label = labels_ref[i] if i >= 0 else before_ref[0, 2 + i]
                utt = utt_ref[i] if i >= 0 else before_ref[1, 2 + i]
                word = jnp.where(utt == utt_ref[at], label, 0)
                around = pl.multiple_of(word // TAG_ROWS * TAG_ROWS, TAG_ROWS)
                n = len(words)
                words.append(word - around)
                copies.insert(n, pltpu.make_async_copy(table.at[pl.ds(around, TAG_ROWS), :], entries.at[n], sems.at[4 + n]))
        *first_copies, weight_copy, q_copy = copies
        for each in copies:
            each.start()
        for peer in range(peers):
            at = peer % CORES * message + CAP * slot_rows
            tile = arrived_ref[peer // CORES, at : at + TAG_ROWS, :].astype(F32)
            tags[peer : peer + 1, :] = tile[:1, :].astype(jnp.int32)
        copy = pltpu.make_async_copy(tags, tag_smem, sems.at[0])
        copy.start()
        copy.wait()
        for peer in range(peers):
            for slot in range(CAP):
                block = tag_smem[peer, slot]
                where[jnp.where(block < 0, count, block)] = peer * CAP + slot

        for each in first_copies:
            each.wait()
        row = lax.broadcasted_iota(jnp.int32, (TAG_ROWS, width), 0)

        def entry(n):
            return jnp.sum(jnp.where(row == words[n], entries[n].astype(F32), 0.0), axis=0, keepdims=True)

        for at in range(2):
            first_rows = (entry(2 * at) + entry(2 * at + 1)).astype(BF16).astype(F32)
            for piece in range(pieces):
                pred_ref[at, piece : piece + 1, :] = first_rows[:, piece * LANES : (piece + 1) * LANES]

        def activate(step):
            for block in range(step * GROUP, (step + 1) * GROUP):
                first = start_ref[block]
                place = where[block]
                chip = place // (CORES * CAP)
                first_row = place // CAP % CORES * message + place % CAP * slot_rows
                for piece in range(pieces):
                    cols = slice(piece * LANES, (piece + 1) * LANES)
                    at = pl.multiple_of(first_row + piece * block_rows, TAG_ROWS)
                    states = arrived_ref[chip, pl.ds(at, block_rows), :].astype(F32)
                    for k in range(S):
                        at = block * out_block + k * block_rows
                        band = pred_ref[first + k, piece : piece + 1, :]
                        act[at : at + block_rows, cols] = jnp.tanh(states + band).astype(BF16)

        def multiply(step):
            if step == 0:
                weight_copy.wait()
            at = slice(step * step_rows, (step + 1) * step_rows)
            logits[at, :] = jnp.dot(act[at, :], weight_ref[...], preferred_element_type=F32)

        def normalise(step):
            if step == 0:
                q_copy.wait()
            for block in range(step * GROUP, (step + 1) * GROUP):
                at = slice(block * out_block, (block + 1) * out_block)
                values = logits[at, :]
                largest = jnp.max(values, axis=-1, keepdims=True)
                total = jnp.sum(jnp.exp(values - largest), axis=-1, keepdims=True)
                mixed = sum(
                    act[at, piece * LANES : (piece + 1) * LANES].astype(F32)
                    * q_ref[at, piece * LANES : (piece + 1) * LANES].astype(F32)
                    for piece in range(pieces)
                )
                mixed = jnp.sum(mixed, axis=-1, keepdims=True)
                sums[...] = jnp.where(lane == block, total, sums[...])
                cross[...] = jnp.where(lane == block, largest - mixed, cross[...])

        for step in range(steps + 2):
            for delay, part in enumerate((activate, multiply, normalise)):
                if 0 <= step - delay < steps:
                    part(step - delay)
        stats = sum(q_ref[total_rows:, part * LANES : (part + 1) * LANES].astype(F32) for part in range(PARTS))
        answers = stats + cross[...].T[:count] + jnp.log(sums[...].T[:count])
        for block in range(count):
            place = where[block]
            owner = place // (CORES * CAP) * CORES + (place // CAP % CORES + core_ref[0]) % CORES
            out_ref[owner, place % CAP] = jnp.broadcast_to(answers[block : block + 1, :], (8, LANES))

    return pl.pallas_call(
        body,
        out_shape=jax.ShapeDtypeStruct((peers, CAP, 8, LANES), F32),
        in_specs=[smem()] * 5 + [vmem()] + [anywhere()] * 5,
        out_specs=vmem(),
        scratch_shapes=[
            pltpu.VMEM((4, TAG_ROWS, width), BF16),
            pltpu.VMEM((total_rows, width), BF16),
            pltpu.VMEM((total_rows, vocab), F32),
            pltpu.VMEM(student_pred.shape, F32),
            pltpu.VMEM((width, vocab), BF16),
            pltpu.VMEM((total_rows + count, width), BF16),
            pltpu.VMEM((peers, LANES), jnp.int32),
            pltpu.SMEM((peers, LANES), jnp.int32),
            pltpu.SMEM((count + 1,), jnp.int32),
            pltpu.VMEM((out_block, LANES), F32),
            pltpu.VMEM((out_block, LANES), F32),
            pltpu.SemaphoreType.DMA((8,)),
        ],
        compiler_params=pltpu.CompilerParams(vmem_limit_bytes=50 << 20),
        cost_estimate=pl.CostEstimate(
            flops=2 * total_rows * width * vocab,
            bytes_accessed=6 << 20,
            transcendentals=total_rows * (width + vocab),
        ),
        name="student",
    )(
        band_start, core, labels, label_utt, before, arrived, student_pred, student_out, q, embed_last, embed_second
    )


def pick(block_list, answers, blocks_per_peer, block_rows):
    count = block_list.shape[1]
    peers = answers.shape[0]

    def body(list_ref, answers_ref, out_ref, used, rows):
        for peer in range(peers):
            used[peer] = 0
        for j in range(count):
            peer = list_ref[0, j] // blocks_per_peer
            slot = used[peer]
            used[peer] = slot + 1
            rows[j : j + 1, :] = answers_ref[peer, slot, :1, :]
        for k in range(S):
            out_ref[:, k, :] = rows[:, k * block_rows : (k + 1) * block_rows]

    return pl.pallas_call(
        body,
        out_shape=jax.ShapeDtypeStruct((count, S, block_rows), F32),
        in_specs=[smem(), vmem()],
        out_specs=vmem(),
        scratch_shapes=[pltpu.SMEM((peers,), jnp.int32), pltpu.VMEM((count, LANES), F32)],
        compiler_params=pltpu.CompilerParams(vmem_limit_bytes=4 << 20),
        name="pick",
    )(block_list, answers)


def shards(
    teacher_states,
    teacher_pred,
    teacher_out,
    student_states,
    embed_last,
    embed_second,
    student_out,
    labels,
    label_utt,
    band_start,
    block_list,
):
    block_count = band_start.shape[0]
    block_rows = student_states.shape[0] // block_count
    frame_peers = lax.axis_size("frames")
    mp_peers = lax.axis_size("mp")
    blocks_per_peer = block_count * mp_peers

    relaid = lax.all_to_all(
        teacher_states.reshape(mp_peers, -1, teacher_states.shape[1]), "mp", split_axis=0, concat_axis=0
    )
    core = jnp.reshape(lax.axis_index("frames") % CORES, (1,)).astype(jnp.int32)
    own, other, student_pred, teacher_tiles, student_out_t = pack(
        block_list, student_states, core, labels[None], label_utt[None], embed_last, embed_second,
        teacher_pred, student_out, frame_peers, blocks_per_peer,
    )
    other = lax.ppermute(other, "frames", [(i, i ^ 1) for i in range(frame_peers)])
    arrived = lax.all_to_all(
        jnp.concatenate([own, other], axis=1),
        "frames", split_axis=0, concat_axis=0,
        axis_index_groups=[list(range(at, frame_peers, CORES)) for at in range(CORES)],
    )

    before = shifted_2(jnp.stack([labels[-2:], label_utt[-2:]]), ("frames", "mp"), 1)
    q = teacher(relaid, teacher_tiles, teacher_out, student_out_t, band_start)
    answers = student(
        core, arrived, student_pred, student_out, band_start, q, labels, label_utt, before, embed_last, embed_second
    )
    returned = lax.all_to_all(answers, "frames", split_axis=0, concat_axis=0)
    return pick(block_list, returned, blocks_per_peer, block_rows)


def solution(mesh):
    placed = (
        P("frames", "mp"),
        P(("frames", "mp"), None),
        P(),
        P(("frames", "mp"), None),
        P(),
        P(),
        P(),
        P(("frames", "mp")),
        P(("frames", "mp")),
        P(("frames", "mp")),
        P(("frames", "mp"), None),
    )
    return jax.shard_map(
        shards,
        mesh=mesh,
        in_specs=placed,
        out_specs=P(("frames", "mp"), None, None),
        check_vma=False,
    )
```

```python
import jax
import jax.numpy as jnp
from jax import lax
from jax.experimental import pallas as pl
from jax.experimental.pallas import tpu as pltpu
from jax.sharding import PartitionSpec as P

S = 4
CAP = 2
LANES = 128
TAG_ROWS = 16
CORES = 2
PARTS = 3
GROUP = 2
BF16 = jnp.bfloat16
F32 = jnp.float32


def shifted_2(block, axis, distance):
    devices = range(lax.axis_size(axis))
    route = [(i - distance, i) for i in devices if i - distance in devices]
    return lax.ppermute(block, axis, route)


def by_tiles(rows, out_ref):
    for piece in range(rows.shape[1] // LANES):
        out_ref[:, piece, :] = rows[:, piece * LANES : (piece + 1) * LANES]


def vmem():
    return pl.BlockSpec(memory_space=pltpu.VMEM)


def hbm():
    return pl.BlockSpec(memory_space=pltpu.HBM)


def anywhere():
    return pl.BlockSpec(memory_space=pl.ANY)


def smem():
    return pl.BlockSpec(memory_space=pltpu.SMEM)


def pack(
    block_list, student_states, core, labels, label_utt, embed_last, embed_second, teacher_pred, student_out,
    frame_peers, blocks_per_peer,
):
    count = block_list.shape[1]
    rows, width = student_states.shape
    block_rows = rows // count
    pieces = width // LANES
    slot_rows = block_rows * pieces
    message = CAP * slot_rows + TAG_ROWS
    chips = frame_peers // CORES
    label_count = labels.shape[1]
    words = embed_last.shape[0]
    assert label_count == LANES

    def body(
        list_ref, core_ref, states_ref, labels_ref, utt_ref, last_ref, second_ref, teacher_pred_ref, student_ref,
        own_ref, other_ref, pred_ref, tiles_ref, turned_ref, used, hot,
    ):
        wide = lax.broadcasted_iota(jnp.int32, (LANES, LANES), 1)

        def embed(distance, ref):
            label = pltpu.roll(jnp.broadcast_to(labels_ref[...], (8, LANES)), distance, 1)
            utt = pltpu.roll(jnp.broadcast_to(utt_ref[...], (8, LANES)), distance, 1)
            label = jnp.where(utt == utt_ref[...], label, 0)
            label = jnp.broadcast_to(label[:1, :].astype(F32), (LANES, LANES)).T.astype(jnp.int32)
            for piece in range(words // LANES):
                cols = slice(piece * LANES, (piece + 1) * LANES)
                hot[:, cols] = (label == wide + piece * LANES).astype(F32).astype(BF16)
            return jnp.dot(hot[...], ref[...], preferred_element_type=F32)

        pred = (embed(1, last_ref) + embed(2, second_ref)).astype(BF16)
        by_tiles(pred.astype(F32), pred_ref)
        by_tiles(teacher_pred_ref[...].astype(F32), tiles_ref)
        turned_ref[...] = student_ref[...].astype(F32).T.astype(BF16)
        lane = lax.broadcasted_iota(jnp.int32, (TAG_ROWS, LANES), 1)
        for peer in range(frame_peers):
            used[peer] = 0
        for chip in range(chips):
            for out_ref in (own_ref, other_ref):
                out_ref[chip, CAP * slot_rows :, :] = jnp.full((TAG_ROWS, LANES), -1.0, BF16)
        for j in range(count):
            block = list_ref[0, j]
            peer = block // blocks_per_peer
            slot = used[peer]
            used[peer] = slot + 1
            local = block % count

            def put(out_ref):
                chip = peer // CORES
                for piece in range(pieces):
                    at = pl.multiple_of(slot * slot_rows + piece * block_rows, TAG_ROWS)
                    out_ref[chip, pl.ds(at, block_rows), :] = states_ref[
                        j * block_rows : (j + 1) * block_rows, piece * LANES : (piece + 1) * LANES
                    ]
                tags = out_ref[chip, CAP * slot_rows :, :].astype(F32)
                tags = jnp.where(lane == slot, local.astype(F32), tags)
                out_ref[chip, CAP * slot_rows :, :] = tags.astype(BF16)

            pl.when(peer % CORES == core_ref[0])(lambda: put(own_ref))
            pl.when(peer % CORES != core_ref[0])(lambda: put(other_ref))

    return pl.pallas_call(
        body,
        out_shape=(jax.ShapeDtypeStruct((chips, message, LANES), BF16),) * 2
        + (
            jax.ShapeDtypeStruct((label_count, pieces, LANES), F32),
            jax.ShapeDtypeStruct((label_count, teacher_pred.shape[1] // LANES, LANES), F32),
            jax.ShapeDtypeStruct(student_out.shape[::-1], BF16),
        ),
        in_specs=[smem(), smem()] + [vmem()] * 7,
        out_specs=(vmem(),) * 5,
        scratch_shapes=[pltpu.SMEM((frame_peers,), jnp.int32), pltpu.VMEM((label_count, words), BF16)],
        compiler_params=pltpu.CompilerParams(vmem_limit_bytes=16 << 20),
        cost_estimate=pl.CostEstimate(flops=0, bytes_accessed=3 << 20, transcendentals=0),
        name="pack",
    )(block_list, core, student_states, labels, label_utt, embed_last, embed_second, teacher_pred, student_out)


def teacher(relaid, teacher_pred, teacher_out, student_out_t, band_start):
    pieces, rows, _ = relaid.shape
    count = band_start.shape[0]
    width, vocab = teacher_out.shape
    student_width = student_out_t.shape[1]
    block_rows = rows // count
    out_block = S * block_rows
    step_rows = GROUP * out_block
    steps = count // GROUP
    total_rows = count * out_block

    def body(start_ref, states_ref, pred_ref, weight_ref, student_ref, q_ref, act, logits, e, inverse, sums, cross):
        lane = lax.broadcasted_iota(jnp.int32, (out_block, LANES), 1)

        def activate(step):
            for block in range(step * GROUP, (step + 1) * GROUP):
                first = start_ref[block]
                for piece in range(pieces):
                    cols = slice(piece * LANES, (piece + 1) * LANES)
                    states = states_ref[piece, block * block_rows : (block + 1) * block_rows, :].astype(F32)
                    for k in range(S):
                        at = block * out_block + k * block_rows
                        band = pred_ref[first + k, piece : piece + 1, :]
                        act[at : at + block_rows, cols] = jnp.tanh(states + band).astype(BF16)

        def multiply(step):
            at = slice(step * step_rows, (step + 1) * step_rows)
            logits[at, :] = jnp.dot(act[at, :], weight_ref[...], preferred_element_type=F32)

        def normalise(step):
            for block in range(step * GROUP, (step + 1) * GROUP):
                at = slice(block * out_block, (block + 1) * out_block)
                values = logits[at, :]
                shifted = values - jnp.max(values, axis=-1, keepdims=True)
                exps = jnp.exp(shifted)
                e[at, :] = exps.astype(BF16)
                total = jnp.sum(exps, axis=-1, keepdims=True)
                weighted = jnp.sum(exps * shifted, axis=-1, keepdims=True)
                inverse[at, :] = jnp.broadcast_to(1.0 / total, (out_block, LANES))
                sums[...] = jnp.where(lane == block, total, sums[...])
                cross[...] = jnp.where(lane == block, weighted, cross[...])

        def project(step):
            at = slice(step * step_rows, (step + 1) * step_rows)
            product = jnp.dot(e[at, :], student_ref[...], preferred_element_type=F32)
            scale = inverse[at, :]
            for piece in range(student_width // LANES):
                cols = slice(piece * LANES, (piece + 1) * LANES)
                q_ref[at, cols] = (product[:, cols] * scale).astype(BF16)

        for step in range(steps + 3):
            for delay, part in enumerate((activate, multiply, normalise, project)):
                if 0 <= step - delay < steps:
                    part(step - delay)
        total = sums[...].T[:count]
        rest = cross[...].T[:count] / total - jnp.log(total)
        for part in range(PARTS):
            rounded = rest.astype(BF16)
            q_ref[total_rows:, part * LANES : (part + 1) * LANES] = rounded
            rest = rest - rounded.astype(F32)

    return pl.pallas_call(
        body,
        out_shape=jax.ShapeDtypeStruct((total_rows + count, student_width), BF16),
        in_specs=[smem(), vmem(), vmem(), vmem(), vmem()],
        out_specs=vmem(),
        scratch_shapes=[
            pltpu.VMEM((total_rows, width), BF16),
            pltpu.VMEM((total_rows, vocab), F32),
            pltpu.VMEM((total_rows, vocab), BF16),
            pltpu.VMEM((total_rows, LANES), F32),
            pltpu.VMEM((out_block, LANES), F32),
            pltpu.VMEM((out_block, LANES), F32),
        ],
        compiler_params=pltpu.CompilerParams(vmem_limit_bytes=56 << 20),
        cost_estimate=pl.CostEstimate(flops=40 << 30, bytes_accessed=8 << 20, transcendentals=0),
        name="teacher",
    )(band_start, relaid, teacher_pred, teacher_out, student_out_t)


def student(
    core, arrived, student_pred, student_out, band_start, q, labels, label_utt, before, embed_last, embed_second
):
    chips, message, _ = arrived.shape
    message //= CORES
    peers = chips * CORES
    count = band_start.shape[0]
    width, vocab = student_out.shape
    pieces = width // LANES
    slot_rows = (message - TAG_ROWS) // CAP
    block_rows = slot_rows // pieces
    out_block = S * block_rows
    step_rows = GROUP * out_block
    steps = count // GROUP
    total_rows = count * out_block
    assert out_block == LANES

    def body(
        start_ref, core_ref, labels_ref, utt_ref, before_ref, arrived_ref, pred_hbm, weight_hbm, q_hbm, last_hbm, second_hbm,
        out_ref, entries,
        act, logits, pred_ref, weight_ref, q_ref, tags, tag_smem, where, sums, cross, sems,
    ):
        lane = lax.broadcasted_iota(jnp.int32, (out_block, LANES), 1)
        copies = [
            pltpu.make_async_copy(pred_hbm, pred_ref, sems.at[1]),
            pltpu.make_async_copy(weight_hbm, weight_ref, sems.at[2]),
            pltpu.make_async_copy(q_hbm, q_ref, sems.at[3]),
        ]
        words = []
        for at in range(2):
            for distance, table in ((1, last_hbm), (2, second_hbm)):
                i = at - distance
                label = labels_ref[i] if i >= 0 else before_ref[0, 2 + i]
                utt = utt_ref[i] if i >= 0 else before_ref[1, 2 + i]
                word = jnp.where(utt == utt_ref[at], label, 0)
                around = pl.multiple_of(word // TAG_ROWS * TAG_ROWS, TAG_ROWS)
                n = len(words)
                words.append(word - around)
                copies.insert(n, pltpu.make_async_copy(table.at[pl.ds(around, TAG_ROWS), :], entries.at[n], sems.at[4 + n]))
        *first_copies, weight_copy, q_copy = copies
        for each in copies:
            each.start()
        for peer in range(peers):
            at = peer % CORES * message + CAP * slot_rows
            tile = arrived_ref[peer // CORES, at : at + TAG_ROWS, :].astype(F32)
            tags[peer : peer + 1, :] = tile[:1, :].astype(jnp.int32)
        copy = pltpu.make_async_copy(tags, tag_smem, sems.at[0])
        copy.start()
        copy.wait()
        for peer in range(peers):
            for slot in range(CAP):
                block = tag_smem[peer, slot]
                where[jnp.where(block < 0, count, block)] = peer * CAP + slot

        for each in first_copies:
            each.wait()
        row = lax.broadcasted_iota(jnp.int32, (TAG_ROWS, width), 0)

        def entry(n):
            return jnp.sum(jnp.where(row == words[n], entries[n].astype(F32), 0.0), axis=0, keepdims=True)

        for at in range(2):
            first_rows = (entry(2 * at) + entry(2 * at + 1)).astype(BF16).astype(F32)
            for piece in range(pieces):
                pred_ref[at, piece : piece + 1, :] = first_rows[:, piece * LANES : (piece + 1) * LANES]

        def activate(step):
            for block in range(step * GROUP, (step + 1) * GROUP):
                first = start_ref[block]
                place = where[block]
                chip = place // (CORES * CAP)
                first_row = place // CAP % CORES * message + place % CAP * slot_rows
                for piece in range(pieces):
                    cols = slice(piece * LANES, (piece + 1) * LANES)
                    at = pl.multiple_of(first_row + piece * block_rows, TAG_ROWS)
                    states = arrived_ref[chip, pl.ds(at, block_rows), :].astype(F32)
                    for k in range(S):
                        at = block * out_block + k * block_rows
                        band = pred_ref[first + k, piece : piece + 1, :]
                        act[at : at + block_rows, cols] = jnp.tanh(states + band).astype(BF16)

        def multiply(step):
            if step == 0:
                weight_copy.wait()
            at = slice(step * step_rows, (step + 1) * step_rows)
            logits[at, :] = jnp.dot(act[at, :], weight_ref[...], preferred_element_type=F32)

        def normalise(step):
            if step == 0:
                q_copy.wait()
            for block in range(step * GROUP, (step + 1) * GROUP):
                at = slice(block * out_block, (block + 1) * out_block)
                values = logits[at, :]
                largest = jnp.max(values, axis=-1, keepdims=True)
                total = jnp.sum(jnp.exp(values - largest), axis=-1, keepdims=True)
                mixed = sum(
                    act[at, piece * LANES : (piece + 1) * LANES].astype(F32)
                    * q_ref[at, piece * LANES : (piece + 1) * LANES].astype(F32)
                    for piece in range(pieces)
                )
                mixed = jnp.sum(mixed, axis=-1, keepdims=True)
                sums[...] = jnp.where(lane == block, total, sums[...])
                cross[...] = jnp.where(lane == block, largest - mixed, cross[...])

        for step in range(steps + 2):
            for delay, part in enumerate((activate, multiply, normalise)):
                if 0 <= step - delay < steps:
                    part(step - delay)
        stats = sum(q_ref[total_rows:, part * LANES : (part + 1) * LANES].astype(F32) for part in range(PARTS))
        answers = stats + cross[...].T[:count] + jnp.log(sums[...].T[:count])
        out_ref[...] = jnp.zeros_like(out_ref)
        slots = lax.broadcasted_iota(jnp.int32, (8, LANES), 0)
        for block in range(count):
            place = where[block]
            owner = place // (CORES * CAP) * CORES + (place // CAP % CORES + core_ref[0]) % CORES
            out_ref[owner] = jnp.where(slots == place % CAP, answers[block : block + 1, :], out_ref[owner])

    return pl.pallas_call(
        body,
        out_shape=jax.ShapeDtypeStruct((peers, 8, LANES), F32),
        in_specs=[smem()] * 5 + [vmem()] + [anywhere()] * 5,
        out_specs=vmem(),
        scratch_shapes=[
            pltpu.VMEM((4, TAG_ROWS, width), BF16),
            pltpu.VMEM((total_rows, width), BF16),
            pltpu.VMEM((total_rows, vocab), F32),
            pltpu.VMEM(student_pred.shape, F32),
            pltpu.VMEM((width, vocab), BF16),
            pltpu.VMEM((total_rows + count, width), BF16),
            pltpu.VMEM((peers, LANES), jnp.int32),
            pltpu.SMEM((peers, LANES), jnp.int32),
            pltpu.SMEM((count + 1,), jnp.int32),
            pltpu.VMEM((out_block, LANES), F32),
            pltpu.VMEM((out_block, LANES), F32),
            pltpu.SemaphoreType.DMA((8,)),
        ],
        compiler_params=pltpu.CompilerParams(vmem_limit_bytes=50 << 20),
        cost_estimate=pl.CostEstimate(
            flops=2 * total_rows * width * vocab,
            bytes_accessed=6 << 20,
            transcendentals=total_rows * (width + vocab),
        ),
        name="student",
    )(
        band_start, core, labels, label_utt, before, arrived, student_pred, student_out, q, embed_last, embed_second
    )


def pick(block_list, answers, blocks_per_peer, block_rows):
    count = block_list.shape[1]
    peers = answers.shape[0]

    def body(list_ref, answers_ref, out_ref, used, rows):
        slots = lax.broadcasted_iota(jnp.int32, (8, LANES), 0)
        for peer in range(peers):
            used[peer] = 0
        for j in range(count):
            peer = list_ref[0, j] // blocks_per_peer
            slot = used[peer]
            used[peer] = slot + 1
            rows[j : j + 1, :] = jnp.sum(jnp.where(slots == slot, answers_ref[peer], 0.0), axis=0, keepdims=True)
        for k in range(S):
            out_ref[:, k, :] = rows[:, k * block_rows : (k + 1) * block_rows]

    return pl.pallas_call(
        body,
        out_shape=jax.ShapeDtypeStruct((count, S, block_rows), F32),
        in_specs=[smem(), vmem()],
        out_specs=vmem(),
        scratch_shapes=[pltpu.SMEM((peers,), jnp.int32), pltpu.VMEM((count, LANES), F32)],
        compiler_params=pltpu.CompilerParams(vmem_limit_bytes=4 << 20),
        name="pick",
    )(block_list, answers)


def shards(
    teacher_states,
    teacher_pred,
    teacher_out,
    student_states,
    embed_last,
    embed_second,
    student_out,
    labels,
    label_utt,
    band_start,
    block_list,
):
    block_count = band_start.shape[0]
    block_rows = student_states.shape[0] // block_count
    frame_peers = lax.axis_size("frames")
    mp_peers = lax.axis_size("mp")
    blocks_per_peer = block_count * mp_peers

    relaid = lax.all_to_all(
        teacher_states.reshape(mp_peers, -1, teacher_states.shape[1]), "mp", split_axis=0, concat_axis=0
    )
    core = jnp.reshape(lax.axis_index("frames") % CORES, (1,)).astype(jnp.int32)
    own, other, student_pred, teacher_tiles, student_out_t = pack(
        block_list, student_states, core, labels[None], label_utt[None], embed_last, embed_second,
        teacher_pred, student_out, frame_peers, blocks_per_peer,
    )
    other = lax.ppermute(other, "frames", [(i, i ^ 1) for i in range(frame_peers)])
    arrived = lax.all_to_all(
        jnp.concatenate([own, other], axis=1),
        "frames", split_axis=0, concat_axis=0,
        axis_index_groups=[list(range(at, frame_peers, CORES)) for at in range(CORES)],
    )

    before = shifted_2(jnp.stack([labels[-2:], label_utt[-2:]]), ("frames", "mp"), 1)
    q = teacher(relaid, teacher_tiles, teacher_out, student_out_t, band_start)
    answers = student(
        core, arrived, student_pred, student_out, band_start, q, labels, label_utt, before, embed_last, embed_second
    )
    returned = lax.all_to_all(answers, "frames", split_axis=0, concat_axis=0)
    return pick(block_list, returned, blocks_per_peer, block_rows)


def solution(mesh):
    placed = (
        P("frames", "mp"),
        P(("frames", "mp"), None),
        P(),
        P(("frames", "mp"), None),
        P(),
        P(),
        P(),
        P(("frames", "mp")),
        P(("frames", "mp")),
        P(("frames", "mp")),
        P(("frames", "mp"), None),
    )
    return jax.shard_map(
        shards,
        mesh=mesh,
        in_specs=placed,
        out_specs=P(("frames", "mp"), None, None),
        check_vma=False,
    )
```

```python
import jax
import jax.numpy as jnp
from jax import lax
from jax.experimental import pallas as pl
from jax.experimental.pallas import tpu as pltpu
from jax.sharding import PartitionSpec as P

S = 4
CAP = 2
LANES = 128
TAG_ROWS = 16
CORES = 2
PARTS = 3
GROUP = 2
BF16 = jnp.bfloat16
F32 = jnp.float32


def shifted_2(block, axis, distance):
    devices = range(lax.axis_size(axis))
    route = [(i - distance, i) for i in devices if i - distance in devices]
    return lax.ppermute(block, axis, route)


def by_tiles(rows, out_ref):
    for piece in range(rows.shape[1] // LANES):
        out_ref[:, piece, :] = rows[:, piece * LANES : (piece + 1) * LANES]


def vmem():
    return pl.BlockSpec(memory_space=pltpu.VMEM)


def hbm():
    return pl.BlockSpec(memory_space=pltpu.HBM)


def anywhere():
    return pl.BlockSpec(memory_space=pl.ANY)


def smem():
    return pl.BlockSpec(memory_space=pltpu.SMEM)


def pack(
    block_list, student_states, core, labels, label_utt, embed_last, embed_second, teacher_pred, student_out,
    frame_peers, blocks_per_peer,
):
    count = block_list.shape[1]
    rows, width = student_states.shape
    block_rows = rows // count
    pieces = width // LANES
    slot_rows = block_rows * pieces
    message = CAP * slot_rows + TAG_ROWS
    chips = frame_peers // CORES
    label_count = labels.shape[1]
    words = embed_last.shape[0]
    assert label_count == LANES

    def body(
        list_ref, core_ref, states_ref, labels_ref, utt_ref, last_ref, second_ref, teacher_pred_ref, student_ref,
        own_ref, other_ref, pred_ref, tiles_ref, turned_ref, used, hot,
    ):
        wide = lax.broadcasted_iota(jnp.int32, (LANES, LANES), 1)

        def embed(distance, ref):
            label = pltpu.roll(jnp.broadcast_to(labels_ref[...], (8, LANES)), distance, 1)
            utt = pltpu.roll(jnp.broadcast_to(utt_ref[...], (8, LANES)), distance, 1)
            label = jnp.where(utt == utt_ref[...], label, 0)
            label = jnp.broadcast_to(label[:1, :].astype(F32), (LANES, LANES)).T.astype(jnp.int32)
            for piece in range(words // LANES):
                cols = slice(piece * LANES, (piece + 1) * LANES)
                hot[:, cols] = (label == wide + piece * LANES).astype(F32).astype(BF16)
            return jnp.dot(hot[...], ref[...], preferred_element_type=F32)

        pred = (embed(1, last_ref) + embed(2, second_ref)).astype(BF16)
        by_tiles(pred.astype(F32), pred_ref)
        by_tiles(teacher_pred_ref[...].astype(F32), tiles_ref)
        turned_ref[...] = student_ref[...].astype(F32).T.astype(BF16)
        lane = lax.broadcasted_iota(jnp.int32, (TAG_ROWS, LANES), 1)
        for peer in range(frame_peers):
            used[peer] = 0
        for chip in range(chips):
            for out_ref in (own_ref, other_ref):
                out_ref[chip, CAP * slot_rows :, :] = jnp.full((TAG_ROWS, LANES), -1.0, BF16)
        for j in range(count):
            block = list_ref[0, j]
            peer = block // blocks_per_peer
            slot = used[peer]
            used[peer] = slot + 1
            local = block % count

            def put(out_ref):
                chip = peer // CORES
                for piece in range(pieces):
                    at = pl.multiple_of(slot * slot_rows + piece * block_rows, TAG_ROWS)
                    out_ref[chip, pl.ds(at, block_rows), :] = states_ref[
                        j * block_rows : (j + 1) * block_rows, piece * LANES : (piece + 1) * LANES
                    ]
                tags = out_ref[chip, CAP * slot_rows :, :].astype(F32)
                tags = jnp.where(lane == slot, local.astype(F32), tags)
                out_ref[chip, CAP * slot_rows :, :] = tags.astype(BF16)

            pl.when(peer % CORES == core_ref[0])(lambda: put(own_ref))
            pl.when(peer % CORES != core_ref[0])(lambda: put(other_ref))

    return pl.pallas_call(
        body,
        out_shape=(jax.ShapeDtypeStruct((chips, message, LANES), BF16),) * 2
        + (
            jax.ShapeDtypeStruct((label_count, pieces, LANES), F32),
            jax.ShapeDtypeStruct((label_count, teacher_pred.shape[1] // LANES, LANES), F32),
            jax.ShapeDtypeStruct(student_out.shape[::-1], BF16),
        ),
        in_specs=[smem(), smem()] + [vmem()] * 7,
        out_specs=(vmem(),) * 5,
        scratch_shapes=[pltpu.SMEM((frame_peers,), jnp.int32), pltpu.VMEM((label_count, words), BF16)],
        compiler_params=pltpu.CompilerParams(vmem_limit_bytes=56 << 20),
        cost_estimate=pl.CostEstimate(flops=0, bytes_accessed=3 << 20, transcendentals=0),
        name="pack",
    )(block_list, core, student_states, labels, label_utt, embed_last, embed_second, teacher_pred, student_out)


def teacher(relaid, teacher_pred, teacher_out, student_out_t, band_start):
    pieces, rows, _ = relaid.shape
    count = band_start.shape[0]
    width, vocab = teacher_out.shape
    student_width = student_out_t.shape[1]
    block_rows = rows // count
    out_block = S * block_rows
    step_rows = GROUP * out_block
    steps = count // GROUP
    total_rows = count * out_block

    def body(start_ref, states_ref, pred_ref, weight_ref, student_ref, q_ref, act, logits, e, inverse, sums, cross):
        lane = lax.broadcasted_iota(jnp.int32, (out_block, LANES), 1)

        def activate(step):
            for block in range(step * GROUP, (step + 1) * GROUP):
                first = start_ref[block]
                for piece in range(pieces):
                    cols = slice(piece * LANES, (piece + 1) * LANES)
                    states = states_ref[piece, block * block_rows : (block + 1) * block_rows, :].astype(F32)
                    for k in range(S):
                        at = block * out_block + k * block_rows
                        band = pred_ref[first + k, piece : piece + 1, :]
                        act[at : at + block_rows, cols] = jnp.tanh(states + band).astype(BF16)

        def multiply(step):
            at = slice(step * step_rows, (step + 1) * step_rows)
            logits[at, :] = jnp.dot(act[at, :], weight_ref[...], preferred_element_type=F32)

        def normalise(step):
            for block in range(step * GROUP, (step + 1) * GROUP):
                at = slice(block * out_block, (block + 1) * out_block)
                values = logits[at, :]
                shifted = values - jnp.max(values, axis=-1, keepdims=True)
                exps = jnp.exp(shifted)
                e[at, :] = exps.astype(BF16)
                total = jnp.sum(exps, axis=-1, keepdims=True)
                weighted = jnp.sum(exps * shifted, axis=-1, keepdims=True)
                inverse[at, :] = jnp.broadcast_to(1.0 / total, (out_block, LANES))
                sums[...] = jnp.where(lane == block, total, sums[...])
                cross[...] = jnp.where(lane == block, weighted, cross[...])

        def project(step):
            at = slice(step * step_rows, (step + 1) * step_rows)
            product = jnp.dot(e[at, :], student_ref[...], preferred_element_type=F32)
            scale = inverse[at, :]
            for piece in range(student_width // LANES):
                cols = slice(piece * LANES, (piece + 1) * LANES)
                q_ref[at, cols] = (product[:, cols] * scale).astype(BF16)

        for step in range(steps + 3):
            for delay, part in enumerate((activate, multiply, normalise, project)):
                if 0 <= step - delay < steps:
                    part(step - delay)
        total = sums[...].T[:count]
        rest = cross[...].T[:count] / total - jnp.log(total)
        for part in range(PARTS):
            rounded = rest.astype(BF16)
            q_ref[total_rows:, part * LANES : (part + 1) * LANES] = rounded
            rest = rest - rounded.astype(F32)

    return pl.pallas_call(
        body,
        out_shape=jax.ShapeDtypeStruct((total_rows + count, student_width), BF16),
        in_specs=[smem(), vmem(), vmem(), vmem(), vmem()],
        out_specs=vmem(),
        scratch_shapes=[
            pltpu.VMEM((total_rows, width), BF16),
            pltpu.VMEM((total_rows, vocab), F32),
            pltpu.VMEM((total_rows, vocab), BF16),
            pltpu.VMEM((total_rows, LANES), F32),
            pltpu.VMEM((out_block, LANES), F32),
            pltpu.VMEM((out_block, LANES), F32),
        ],
        compiler_params=pltpu.CompilerParams(vmem_limit_bytes=56 << 20),
        cost_estimate=pl.CostEstimate(flops=40 << 30, bytes_accessed=8 << 20, transcendentals=0),
        name="teacher",
    )(band_start, relaid, teacher_pred, teacher_out, student_out_t)


def student(
    core, arrived, student_pred, student_out, band_start, q, labels, label_utt, before, embed_last, embed_second
):
    chips, message, _ = arrived.shape
    message //= CORES
    peers = chips * CORES
    count = band_start.shape[0]
    width, vocab = student_out.shape
    pieces = width // LANES
    slot_rows = (message - TAG_ROWS) // CAP
    block_rows = slot_rows // pieces
    out_block = S * block_rows
    step_rows = GROUP * out_block
    steps = count // GROUP
    total_rows = count * out_block
    assert out_block == LANES

    def body(
        start_ref, core_ref, labels_ref, utt_ref, before_ref, arrived_ref, pred_hbm, weight_hbm, q_hbm, last_hbm, second_hbm,
        out_ref, entries,
        act, logits, pred_ref, weight_ref, q_ref, tags, tag_smem, where, sums, cross, sems,
    ):
        lane = lax.broadcasted_iota(jnp.int32, (out_block, LANES), 1)
        copies = [
            pltpu.make_async_copy(pred_hbm, pred_ref, sems.at[1]),
            pltpu.make_async_copy(weight_hbm, weight_ref, sems.at[2]),
            pltpu.make_async_copy(q_hbm, q_ref, sems.at[3]),
        ]
        words = []
        for at in range(2):
            for distance, table in ((1, last_hbm), (2, second_hbm)):
                i = at - distance
                label = labels_ref[i] if i >= 0 else before_ref[0, 2 + i]
                utt = utt_ref[i] if i >= 0 else before_ref[1, 2 + i]
                word = jnp.where(utt == utt_ref[at], label, 0)
                around = pl.multiple_of(word // TAG_ROWS * TAG_ROWS, TAG_ROWS)
                n = len(words)
                words.append(word - around)
                copies.insert(n, pltpu.make_async_copy(table.at[pl.ds(around, TAG_ROWS), :], entries.at[n], sems.at[4 + n]))
        *first_copies, weight_copy, q_copy = copies
        for peer in range(peers):
            at = peer % CORES * message + CAP * slot_rows
            tile = arrived_ref[peer // CORES, at : at + TAG_ROWS, :].astype(F32)
            tags[peer : peer + 1, :] = tile[:1, :].astype(jnp.int32)
        copy = pltpu.make_async_copy(tags, tag_smem, sems.at[0])
        copy.start()
        for each in copies:
            each.start()
        copy.wait()
        for peer in range(peers):
            for slot in range(CAP):
                block = tag_smem[peer, slot]
                where[jnp.where(block < 0, count, block)] = peer * CAP + slot

        for each in first_copies:
            each.wait()
        row = lax.broadcasted_iota(jnp.int32, (TAG_ROWS, width), 0)

        def entry(n):
            return jnp.sum(jnp.where(row == words[n], entries[n].astype(F32), 0.0), axis=0, keepdims=True)

        for at in range(2):
            first_rows = (entry(2 * at) + entry(2 * at + 1)).astype(BF16).astype(F32)
            for piece in range(pieces):
                pred_ref[at, piece : piece + 1, :] = first_rows[:, piece * LANES : (piece + 1) * LANES]

        def activate(step):
            for block in range(step * GROUP, (step + 1) * GROUP):
                first = start_ref[block]
                place = where[block]
                chip = place // (CORES * CAP)
                first_row = place // CAP % CORES * message + place % CAP * slot_rows
                for piece in range(pieces):
                    cols = slice(piece * LANES, (piece + 1) * LANES)
                    at = pl.multiple_of(first_row + piece * block_rows, TAG_ROWS)
                    states = arrived_ref[chip, pl.ds(at, block_rows), :].astype(F32)
                    for k in range(S):
                        at = block * out_block + k * block_rows
                        band = pred_ref[first + k, piece : piece + 1, :]
                        act[at : at + block_rows, cols] = jnp.tanh(states + band).astype(BF16)

        def multiply(step):
            if step == 0:
                weight_copy.wait()
            at = slice(step * step_rows, (step + 1) * step_rows)
            logits[at, :] = jnp.dot(act[at, :], weight_ref[...], preferred_element_type=F32)

        def normalise(step):
            if step == 0:
                q_copy.wait()
            for block in range(step * GROUP, (step + 1) * GROUP):
                at = slice(block * out_block, (block + 1) * out_block)
                values = logits[at, :]
                largest = jnp.max(values, axis=-1, keepdims=True)
                total = jnp.sum(jnp.exp(values - largest), axis=-1, keepdims=True)
                mixed = sum(
                    act[at, piece * LANES : (piece + 1) * LANES].astype(F32)
                    * q_ref[at, piece * LANES : (piece + 1) * LANES].astype(F32)
                    for piece in range(pieces)
                )
                mixed = jnp.sum(mixed, axis=-1, keepdims=True)
                sums[...] = jnp.where(lane == block, total, sums[...])
                cross[...] = jnp.where(lane == block, largest - mixed, cross[...])

        for step in range(steps + 2):
            for delay, part in enumerate((activate, multiply, normalise)):
                if 0 <= step - delay < steps:
                    part(step - delay)
        stats = sum(q_ref[total_rows:, part * LANES : (part + 1) * LANES].astype(F32) for part in range(PARTS))
        answers = stats + cross[...].T[:count] + jnp.log(sums[...].T[:count])
        out_ref[...] = jnp.zeros_like(out_ref)
        slots = lax.broadcasted_iota(jnp.int32, (8, LANES), 0)
        for block in range(count):
            place = where[block]
            owner = place // (CORES * CAP) * CORES + (place // CAP % CORES + core_ref[0]) % CORES
            out_ref[owner] = jnp.where(slots == place % CAP, answers[block : block + 1, :], out_ref[owner])

    return pl.pallas_call(
        body,
        out_shape=jax.ShapeDtypeStruct((peers, 8, LANES), F32),
        in_specs=[smem()] * 5 + [vmem()] + [anywhere()] * 5,
        out_specs=vmem(),
        scratch_shapes=[
            pltpu.VMEM((4, TAG_ROWS, width), BF16),
            pltpu.VMEM((total_rows, width), BF16),
            pltpu.VMEM((total_rows, vocab), F32),
            pltpu.VMEM(student_pred.shape, F32),
            pltpu.VMEM((width, vocab), BF16),
            pltpu.VMEM((total_rows + count, width), BF16),
            pltpu.VMEM((peers, LANES), jnp.int32),
            pltpu.SMEM((peers, LANES), jnp.int32),
            pltpu.SMEM((count + 1,), jnp.int32),
            pltpu.VMEM((out_block, LANES), F32),
            pltpu.VMEM((out_block, LANES), F32),
            pltpu.SemaphoreType.DMA((8,)),
        ],
        compiler_params=pltpu.CompilerParams(vmem_limit_bytes=50 << 20),
        cost_estimate=pl.CostEstimate(
            flops=2 * total_rows * width * vocab,
            bytes_accessed=6 << 20,
            transcendentals=total_rows * (width + vocab),
        ),
        name="student",
    )(
        band_start, core, labels, label_utt, before, arrived, student_pred, student_out, q, embed_last, embed_second
    )


def pick(block_list, answers, blocks_per_peer, block_rows):
    count = block_list.shape[1]
    peers = answers.shape[0]

    def body(list_ref, answers_ref, out_ref, used, rows):
        slots = lax.broadcasted_iota(jnp.int32, (8, LANES), 0)
        for peer in range(peers):
            used[peer] = 0
        for j in range(count):
            peer = list_ref[0, j] // blocks_per_peer
            slot = used[peer]
            used[peer] = slot + 1
            rows[j : j + 1, :] = jnp.sum(jnp.where(slots == slot, answers_ref[peer], 0.0), axis=0, keepdims=True)
        for k in range(S):
            out_ref[:, k, :] = rows[:, k * block_rows : (k + 1) * block_rows]

    return pl.pallas_call(
        body,
        out_shape=jax.ShapeDtypeStruct((count, S, block_rows), F32),
        in_specs=[smem(), vmem()],
        out_specs=vmem(),
        scratch_shapes=[pltpu.SMEM((peers,), jnp.int32), pltpu.VMEM((count, LANES), F32)],
        compiler_params=pltpu.CompilerParams(vmem_limit_bytes=4 << 20),
        name="pick",
    )(block_list, answers)


def shards(
    teacher_states,
    teacher_pred,
    teacher_out,
    student_states,
    embed_last,
    embed_second,
    student_out,
    labels,
    label_utt,
    band_start,
    block_list,
):
    block_count = band_start.shape[0]
    block_rows = student_states.shape[0] // block_count
    frame_peers = lax.axis_size("frames")
    mp_peers = lax.axis_size("mp")
    blocks_per_peer = block_count * mp_peers

    relaid = lax.all_to_all(
        teacher_states.reshape(mp_peers, -1, teacher_states.shape[1]), "mp", split_axis=0, concat_axis=0
    )
    core = jnp.reshape(lax.axis_index("frames") % CORES, (1,)).astype(jnp.int32)
    own, other, student_pred, teacher_tiles, student_out_t = pack(
        block_list, student_states, core, labels[None], label_utt[None], embed_last, embed_second,
        teacher_pred, student_out, frame_peers, blocks_per_peer,
    )
    other = lax.ppermute(other, "frames", [(i, i ^ 1) for i in range(frame_peers)])
    arrived = lax.all_to_all(
        jnp.concatenate([own, other], axis=1),
        "frames", split_axis=0, concat_axis=0,
        axis_index_groups=[list(range(at, frame_peers, CORES)) for at in range(CORES)],
    )

    before = shifted_2(jnp.stack([labels[-2:], label_utt[-2:]]), ("frames", "mp"), 1)
    q = teacher(relaid, teacher_tiles, teacher_out, student_out_t, band_start)
    answers = student(
        core, arrived, student_pred, student_out, band_start, q, labels, label_utt, before, embed_last, embed_second
    )
    returned = lax.all_to_all(answers, "frames", split_axis=0, concat_axis=0)
    return pick(block_list, returned, blocks_per_peer, block_rows)


def solution(mesh):
    placed = (
        P("frames", "mp"),
        P(("frames", "mp"), None),
        P(),
        P(("frames", "mp"), None),
        P(),
        P(),
        P(),
        P(("frames", "mp")),
        P(("frames", "mp")),
        P(("frames", "mp")),
        P(("frames", "mp"), None),
    )
    return jax.shard_map(
        shards,
        mesh=mesh,
        in_specs=placed,
        out_specs=P(("frames", "mp"), None, None),
        check_vma=False,
    )
```

```python
import jax
import jax.numpy as jnp
from jax import lax
from jax.experimental import pallas as pl
from jax.experimental.pallas import tpu as pltpu
from jax.sharding import PartitionSpec as P

S = 4
CAP = 2
LANES = 128
TAG_ROWS = 16
CORES = 2
PARTS = 3
GROUP = 2
STUDENT_GROUP = 4
BF16 = jnp.bfloat16
F32 = jnp.float32


def shifted_2(block, axis, distance):
    devices = range(lax.axis_size(axis))
    route = [(i - distance, i) for i in devices if i - distance in devices]
    return lax.ppermute(block, axis, route)


def by_tiles(rows, out_ref):
    for piece in range(rows.shape[1] // LANES):
        out_ref[:, piece, :] = rows[:, piece * LANES : (piece + 1) * LANES]


def vmem():
    return pl.BlockSpec(memory_space=pltpu.VMEM)


def hbm():
    return pl.BlockSpec(memory_space=pltpu.HBM)


def anywhere():
    return pl.BlockSpec(memory_space=pl.ANY)


def smem():
    return pl.BlockSpec(memory_space=pltpu.SMEM)


def pack(
    block_list, student_states, core, labels, label_utt, embed_last, embed_second, teacher_pred, student_out,
    frame_peers, blocks_per_peer,
):
    count = block_list.shape[1]
    rows, width = student_states.shape
    block_rows = rows // count
    pieces = width // LANES
    slot_rows = block_rows * pieces
    message = CAP * slot_rows + TAG_ROWS
    chips = frame_peers // CORES
    label_count = labels.shape[1]
    words = embed_last.shape[0]
    assert label_count == LANES

    def body(
        list_ref, core_ref, states_ref, labels_ref, utt_ref, last_ref, second_ref, teacher_pred_ref, student_ref,
        own_ref, other_ref, pred_ref, tiles_ref, turned_ref, used, hot,
    ):
        wide = lax.broadcasted_iota(jnp.int32, (LANES, LANES), 1)

        def embed(distance, ref):
            label = pltpu.roll(jnp.broadcast_to(labels_ref[...], (8, LANES)), distance, 1)
            utt = pltpu.roll(jnp.broadcast_to(utt_ref[...], (8, LANES)), distance, 1)
            label = jnp.where(utt == utt_ref[...], label, 0)
            label = jnp.broadcast_to(label[:1, :].astype(F32), (LANES, LANES)).T.astype(jnp.int32)
            for piece in range(words // LANES):
                cols = slice(piece * LANES, (piece + 1) * LANES)
                hot[:, cols] = (label == wide + piece * LANES).astype(F32).astype(BF16)
            return jnp.dot(hot[...], ref[...], preferred_element_type=F32)

        pred = (embed(1, last_ref) + embed(2, second_ref)).astype(BF16)
        by_tiles(pred.astype(F32), pred_ref)
        by_tiles(teacher_pred_ref[...].astype(F32), tiles_ref)
        turned_ref[...] = student_ref[...].astype(F32).T.astype(BF16)
        lane = lax.broadcasted_iota(jnp.int32, (TAG_ROWS, LANES), 1)
        for peer in range(frame_peers):
            used[peer] = 0
        for chip in range(chips):
            for out_ref in (own_ref, other_ref):
                out_ref[chip, CAP * slot_rows :, :] = jnp.full((TAG_ROWS, LANES), -1.0, BF16)
        for j in range(count):
            block = list_ref[0, j]
            peer = block // blocks_per_peer
            slot = used[peer]
            used[peer] = slot + 1
            local = block % count

            def put(out_ref):
                chip = peer // CORES
                for piece in range(pieces):
                    at = pl.multiple_of(slot * slot_rows + piece * block_rows, TAG_ROWS)
                    out_ref[chip, pl.ds(at, block_rows), :] = states_ref[
                        j * block_rows : (j + 1) * block_rows, piece * LANES : (piece + 1) * LANES
                    ]
                tags = out_ref[chip, CAP * slot_rows :, :].astype(F32)
                tags = jnp.where(lane == slot, local.astype(F32), tags)
                out_ref[chip, CAP * slot_rows :, :] = tags.astype(BF16)

            pl.when(peer % CORES == core_ref[0])(lambda: put(own_ref))
            pl.when(peer % CORES != core_ref[0])(lambda: put(other_ref))

    return pl.pallas_call(
        body,
        out_shape=(jax.ShapeDtypeStruct((chips, message, LANES), BF16),) * 2
        + (
            jax.ShapeDtypeStruct((label_count, pieces, LANES), F32),
            jax.ShapeDtypeStruct((label_count, teacher_pred.shape[1] // LANES, LANES), F32),
            jax.ShapeDtypeStruct(student_out.shape[::-1], BF16),
        ),
        in_specs=[smem(), smem()] + [vmem()] * 7,
        out_specs=(vmem(),) * 5,
        scratch_shapes=[pltpu.SMEM((frame_peers,), jnp.int32), pltpu.VMEM((label_count, words), BF16)],
        compiler_params=pltpu.CompilerParams(vmem_limit_bytes=56 << 20),
        cost_estimate=pl.CostEstimate(flops=0, bytes_accessed=3 << 20, transcendentals=0),
        name="pack",
    )(block_list, core, student_states, labels, label_utt, embed_last, embed_second, teacher_pred, student_out)


def teacher(relaid, teacher_pred, teacher_out, student_out_t, band_start):
    pieces, rows, _ = relaid.shape
    count = band_start.shape[0]
    width, vocab = teacher_out.shape
    student_width = student_out_t.shape[1]
    block_rows = rows // count
    out_block = S * block_rows
    step_rows = GROUP * out_block
    steps = count // GROUP
    total_rows = count * out_block

    def body(start_ref, states_ref, pred_ref, weight_ref, student_ref, q_ref, act, logits, e, inverse, sums, cross):
        lane = lax.broadcasted_iota(jnp.int32, (out_block, LANES), 1)

        def activate(step):
            for block in range(step * GROUP, (step + 1) * GROUP):
                first = start_ref[block]
                for piece in range(pieces):
                    cols = slice(piece * LANES, (piece + 1) * LANES)
                    states = states_ref[piece, block * block_rows : (block + 1) * block_rows, :].astype(F32)
                    for k in range(S):
                        at = block * out_block + k * block_rows
                        band = pred_ref[first + k, piece : piece + 1, :]
                        act[at : at + block_rows, cols] = jnp.tanh(states + band).astype(BF16)

        def multiply(step):
            at = slice(step * step_rows, (step + 1) * step_rows)
            logits[at, :] = jnp.dot(act[at, :], weight_ref[...], preferred_element_type=F32)

        def normalise(step):
            for block in range(step * GROUP, (step + 1) * GROUP):
                at = slice(block * out_block, (block + 1) * out_block)
                values = logits[at, :]
                shifted = values - jnp.max(values, axis=-1, keepdims=True)
                exps = jnp.exp(shifted)
                e[at, :] = exps.astype(BF16)
                total = jnp.sum(exps, axis=-1, keepdims=True)
                weighted = jnp.sum(exps * shifted, axis=-1, keepdims=True)
                inverse[at, :] = jnp.broadcast_to(1.0 / total, (out_block, LANES))
                sums[...] = jnp.where(lane == block, total, sums[...])
                cross[...] = jnp.where(lane == block, weighted, cross[...])

        def project(step):
            at = slice(step * step_rows, (step + 1) * step_rows)
            product = jnp.dot(e[at, :], student_ref[...], preferred_element_type=F32)
            scale = inverse[at, :]
            for piece in range(student_width // LANES):
                cols = slice(piece * LANES, (piece + 1) * LANES)
                q_ref[at, cols] = (product[:, cols] * scale).astype(BF16)

        for step in range(steps + 3):
            for delay, part in enumerate((activate, multiply, normalise, project)):
                if 0 <= step - delay < steps:
                    part(step - delay)
        total = sums[...].T[:count]
        rest = cross[...].T[:count] / total - jnp.log(total)
        for part in range(PARTS):
            rounded = rest.astype(BF16)
            q_ref[total_rows:, part * LANES : (part + 1) * LANES] = rounded
            rest = rest - rounded.astype(F32)

    return pl.pallas_call(
        body,
        out_shape=jax.ShapeDtypeStruct((total_rows + count, student_width), BF16),
        in_specs=[smem(), vmem(), vmem(), vmem(), vmem()],
        out_specs=vmem(),
        scratch_shapes=[
            pltpu.VMEM((total_rows, width), BF16),
            pltpu.VMEM((total_rows, vocab), F32),
            pltpu.VMEM((total_rows, vocab), BF16),
            pltpu.VMEM((total_rows, LANES), F32),
            pltpu.VMEM((out_block, LANES), F32),
            pltpu.VMEM((out_block, LANES), F32),
        ],
        compiler_params=pltpu.CompilerParams(vmem_limit_bytes=56 << 20),
        cost_estimate=pl.CostEstimate(flops=40 << 30, bytes_accessed=8 << 20, transcendentals=0),
        name="teacher",
    )(band_start, relaid, teacher_pred, teacher_out, student_out_t)


def student(
    core, arrived, student_pred, student_out, band_start, q, labels, label_utt, before, embed_last, embed_second
):
    chips, message, _ = arrived.shape
    message //= CORES
    peers = chips * CORES
    count = band_start.shape[0]
    width, vocab = student_out.shape
    pieces = width // LANES
    slot_rows = (message - TAG_ROWS) // CAP
    block_rows = slot_rows // pieces
    out_block = S * block_rows
    step_rows = STUDENT_GROUP * out_block
    steps = count // STUDENT_GROUP
    total_rows = count * out_block
    assert out_block == LANES

    def body(
        start_ref, core_ref, labels_ref, utt_ref, before_ref, arrived_ref, pred_hbm, weight_hbm, q_hbm, last_hbm, second_hbm,
        out_ref, entries,
        act, logits, pred_ref, weight_ref, q_ref, tags, tag_smem, where, sums, cross, sems,
    ):
        lane = lax.broadcasted_iota(jnp.int32, (out_block, LANES), 1)
        copies = [
            pltpu.make_async_copy(pred_hbm, pred_ref, sems.at[1]),
            pltpu.make_async_copy(weight_hbm, weight_ref, sems.at[2]),
            pltpu.make_async_copy(q_hbm, q_ref, sems.at[3]),
        ]
        words = []
        for at in range(2):
            for distance, table in ((1, last_hbm), (2, second_hbm)):
                i = at - distance
                label = labels_ref[i] if i >= 0 else before_ref[0, 2 + i]
                utt = utt_ref[i] if i >= 0 else before_ref[1, 2 + i]
                word = jnp.where(utt == utt_ref[at], label, 0)
                around = pl.multiple_of(word // TAG_ROWS * TAG_ROWS, TAG_ROWS)
                n = len(words)
                words.append(word - around)
                copies.insert(n, pltpu.make_async_copy(table.at[pl.ds(around, TAG_ROWS), :], entries.at[n], sems.at[4 + n]))
        *first_copies, weight_copy, q_copy = copies
        for peer in range(peers):
            at = peer % CORES * message + CAP * slot_rows
            tile = arrived_ref[peer // CORES, at : at + TAG_ROWS, :].astype(F32)
            tags[peer : peer + 1, :] = tile[:1, :].astype(jnp.int32)
        copy = pltpu.make_async_copy(tags, tag_smem, sems.at[0])
        copy.start()
        for each in copies:
            each.start()
        copy.wait()
        for peer in range(peers):
            for slot in range(CAP):
                block = tag_smem[peer, slot]
                where[jnp.where(block < 0, count, block)] = peer * CAP + slot

        for each in first_copies:
            each.wait()
        row = lax.broadcasted_iota(jnp.int32, (TAG_ROWS, width), 0)

        def entry(n):
            return jnp.sum(jnp.where(row == words[n], entries[n].astype(F32), 0.0), axis=0, keepdims=True)

        for at in range(2):
            first_rows = (entry(2 * at) + entry(2 * at + 1)).astype(BF16).astype(F32)
            for piece in range(pieces):
                pred_ref[at, piece : piece + 1, :] = first_rows[:, piece * LANES : (piece + 1) * LANES]

        def activate(step):
            for block in range(step * STUDENT_GROUP, (step + 1) * STUDENT_GROUP):
                first = start_ref[block]
                place = where[block]
                chip = place // (CORES * CAP)
                first_row = place // CAP % CORES * message + place % CAP * slot_rows
                for piece in range(pieces):
                    cols = slice(piece * LANES, (piece + 1) * LANES)
                    at = pl.multiple_of(first_row + piece * block_rows, TAG_ROWS)
                    states = arrived_ref[chip, pl.ds(at, block_rows), :].astype(F32)
                    for k in range(S):
                        at = block * out_block + k * block_rows
                        band = pred_ref[first + k, piece : piece + 1, :]
                        act[at : at + block_rows, cols] = jnp.tanh(states + band).astype(BF16)

        def multiply(step):
            if step == 0:
                weight_copy.wait()
            at = slice(step * step_rows, (step + 1) * step_rows)
            logits[at, :] = jnp.dot(act[at, :], weight_ref[...], preferred_element_type=F32)

        def normalise(step):
            if step == 0:
                q_copy.wait()
            for block in range(step * STUDENT_GROUP, (step + 1) * STUDENT_GROUP):
                at = slice(block * out_block, (block + 1) * out_block)
                values = logits[at, :]
                largest = jnp.max(values, axis=-1, keepdims=True)
                total = jnp.sum(jnp.exp(values - largest), axis=-1, keepdims=True)
                mixed = sum(
                    act[at, piece * LANES : (piece + 1) * LANES].astype(F32)
                    * q_ref[at, piece * LANES : (piece + 1) * LANES].astype(F32)
                    for piece in range(pieces)
                )
                mixed = jnp.sum(mixed, axis=-1, keepdims=True)
                sums[...] = jnp.where(lane == block, total, sums[...])
                cross[...] = jnp.where(lane == block, largest - mixed, cross[...])

        for step in range(steps + 2):
            for delay, part in enumerate((activate, multiply, normalise)):
                if 0 <= step - delay < steps:
                    part(step - delay)
        stats = sum(q_ref[total_rows:, part * LANES : (part + 1) * LANES].astype(F32) for part in range(PARTS))
        answers = stats + cross[...].T[:count] + jnp.log(sums[...].T[:count])
        out_ref[...] = jnp.zeros_like(out_ref)
        slots = lax.broadcasted_iota(jnp.int32, (8, LANES), 0)
        for block in range(count):
            place = where[block]
            owner = place // (CORES * CAP) * CORES + (place // CAP % CORES + core_ref[0]) % CORES
            out_ref[owner] = jnp.where(slots == place % CAP, answers[block : block + 1, :], out_ref[owner])

    return pl.pallas_call(
        body,
        out_shape=jax.ShapeDtypeStruct((peers, 8, LANES), F32),
        in_specs=[smem()] * 5 + [vmem()] + [anywhere()] * 5,
        out_specs=vmem(),
        scratch_shapes=[
            pltpu.VMEM((4, TAG_ROWS, width), BF16),
            pltpu.VMEM((total_rows, width), BF16),
            pltpu.VMEM((total_rows, vocab), F32),
            pltpu.VMEM(student_pred.shape, F32),
            pltpu.VMEM((width, vocab), BF16),
            pltpu.VMEM((total_rows + count, width), BF16),
            pltpu.VMEM((peers, LANES), jnp.int32),
            pltpu.SMEM((peers, LANES), jnp.int32),
            pltpu.SMEM((count + 1,), jnp.int32),
            pltpu.VMEM((out_block, LANES), F32),
            pltpu.VMEM((out_block, LANES), F32),
            pltpu.SemaphoreType.DMA((8,)),
        ],
        compiler_params=pltpu.CompilerParams(vmem_limit_bytes=50 << 20),
        cost_estimate=pl.CostEstimate(
            flops=2 * total_rows * width * vocab,
            bytes_accessed=6 << 20,
            transcendentals=total_rows * (width + vocab),
        ),
        name="student",
    )(
        band_start, core, labels, label_utt, before, arrived, student_pred, student_out, q, embed_last, embed_second
    )


def pick(block_list, answers, blocks_per_peer, block_rows):
    count = block_list.shape[1]
    peers = answers.shape[0]

    def body(list_ref, answers_ref, out_ref, used, rows):
        slots = lax.broadcasted_iota(jnp.int32, (8, LANES), 0)
        for peer in range(peers):
            used[peer] = 0
        for j in range(count):
            peer = list_ref[0, j] // blocks_per_peer
            slot = used[peer]
            used[peer] = slot + 1
            rows[j : j + 1, :] = jnp.sum(jnp.where(slots == slot, answers_ref[peer], 0.0), axis=0, keepdims=True)
        for k in range(S):
            out_ref[:, k, :] = rows[:, k * block_rows : (k + 1) * block_rows]

    return pl.pallas_call(
        body,
        out_shape=jax.ShapeDtypeStruct((count, S, block_rows), F32),
        in_specs=[smem(), vmem()],
        out_specs=vmem(),
        scratch_shapes=[pltpu.SMEM((peers,), jnp.int32), pltpu.VMEM((count, LANES), F32)],
        compiler_params=pltpu.CompilerParams(vmem_limit_bytes=4 << 20),
        name="pick",
    )(block_list, answers)


def shards(
    teacher_states,
    teacher_pred,
    teacher_out,
    student_states,
    embed_last,
    embed_second,
    student_out,
    labels,
    label_utt,
    band_start,
    block_list,
):
    block_count = band_start.shape[0]
    block_rows = student_states.shape[0] // block_count
    frame_peers = lax.axis_size("frames")
    mp_peers = lax.axis_size("mp")
    blocks_per_peer = block_count * mp_peers

    relaid = lax.all_to_all(
        teacher_states.reshape(mp_peers, -1, teacher_states.shape[1]), "mp", split_axis=0, concat_axis=0
    )
    core = jnp.reshape(lax.axis_index("frames") % CORES, (1,)).astype(jnp.int32)
    own, other, student_pred, teacher_tiles, student_out_t = pack(
        block_list, student_states, core, labels[None], label_utt[None], embed_last, embed_second,
        teacher_pred, student_out, frame_peers, blocks_per_peer,
    )
    other = lax.ppermute(other, "frames", [(i, i ^ 1) for i in range(frame_peers)])
    arrived = lax.all_to_all(
        jnp.concatenate([own, other], axis=1),
        "frames", split_axis=0, concat_axis=0,
        axis_index_groups=[list(range(at, frame_peers, CORES)) for at in range(CORES)],
    )

    before = shifted_2(jnp.stack([labels[-2:], label_utt[-2:]]), ("frames", "mp"), 1)
    q = teacher(relaid, teacher_tiles, teacher_out, student_out_t, band_start)
    answers = student(
        core, arrived, student_pred, student_out, band_start, q, labels, label_utt, before, embed_last, embed_second
    )
    returned = lax.all_to_all(answers, "frames", split_axis=0, concat_axis=0)
    return pick(block_list, returned, blocks_per_peer, block_rows)


def solution(mesh):
    placed = (
        P("frames", "mp"),
        P(("frames", "mp"), None),
        P(),
        P(("frames", "mp"), None),
        P(),
        P(),
        P(),
        P(("frames", "mp")),
        P(("frames", "mp")),
        P(("frames", "mp")),
        P(("frames", "mp"), None),
    )
    return jax.shard_map(
        shards,
        mesh=mesh,
        in_specs=placed,
        out_specs=P(("frames", "mp"), None, None),
        check_vma=False,
    )
```
